256 devices in a mesh: seq: 128 (over y_hi, x, z, core), ch: 2 (over y_lo).
Axes of the slice: x: 4, y: 4 (y_hi: 2, y_lo: 2; y = y_hi * 2 + y_lo), z: 8, core: 2. Of those that a mesh axis runs over, the one named last changes fastest.
Arguments:
- gated: bfloat16 [4096, 16384], P('ch', 'seq'), may hold values from -6 to 6
- value: bfloat16 [4096, 16384], P('ch', 'seq'), may hold values from -6 to 6
- upstream: bfloat16 [4096, 16384], P('ch', 'seq'), may hold values from -6 to 6
- residue: float32 [4096, 16], replicated, may hold values from -0.078125 to 0.078125
- rate: float32 [4096, 16], replicated, may hold values from 3.0517578e-06 to 0.0333333333
- skip_weight: float32 [4096], replicated, may hold values from -6 to 6
Outputs:
- grad_gated: bfloat16 [4096, 16384], P('ch', 'seq')
- grad_value: bfloat16 [4096, 16384], P('ch', 'seq')
- grad_residue: float32 [4096, 16], replicated
The draws below stay inside these ranges and needn't reach their ends.
All inputs are finite; a program needn't handle non-finite values.
Results may differ from the reference program's by a relative error of at most 0.0051.
Values may be sent and summed in bfloat16 or wider, within the bound.
No kernel may reach another device: no remote copies, remote signals or barrier semaphores. Data moves between devices by JAX's collectives and lax.ppermute only.
A program may use at most 128 MiB of HBM per device.

```python
import math
import jax
import jax.numpy as jnp
from jax import lax

D = 4096
M = 16
TOKENS = 16384


def draw_rate(key, part):
    key = jax.random.fold_in(key, 11)
    fractions = jax.random.uniform(key, (D, M), jnp.float32)
    lowest = 0.3 / TOKENS
    highest = 1.0 / 30.0
    return jnp.exp(math.log(lowest) + fractions * (math.log(highest) - math.log(lowest)))


def level_of(stream_key, shape, shards, least, top_value):
    factor_of, own = 1.0, jax.random.fold_in(stream_key, 6)
    for dim, parts in shards:
        draws = jnp.exp(jax.random.uniform(jax.random.fold_in(own, dim), (parts,), jnp.float32, least / len(shards), top_value / len(shards)))
        factor_of = factor_of * jnp.repeat(draws, shape[dim] // parts).reshape([-1 if axis == dim else 1 for axis in range(len(shape))])
    return factor_of


def centred(own_key, extent, spread, bound, pieces=(), kind=jnp.bfloat16):
    level = level_of(own_key, extent, pieces, -0.22, 0.18) if pieces else 1.0
    values = jax.random.normal(own_key, extent, jnp.float32) * spread * level
    return jnp.minimum(jnp.maximum(values, -bound), bound).astype(kind)


def setup_inputs(seed: int = 0) -> dict:
    keys = jax.random.split(jax.random.key(seed), 7)
    return {
        "gated": centred(keys[0], (D, TOKENS), 1.0, 6.0, ((0, 2), (1, 128))),
        "value": centred(keys[1], (D, TOKENS), 1.0, 6.0, ((0, 2), (1, 128))),
        "upstream": centred(keys[2], (D, TOKENS), 1.0, 6.0, ((0, 2), (1, 128))),
        "residue": centred(keys[3], (D, M), ((8.0 / (M * TOKENS)) ** 0.5), 0.078125, (), jnp.float32),
        "rate": draw_rate(jax.random.fold_in(keys[6], 71), 0),
        "skip_weight": centred(keys[5], (D,), 1.0, 6.0, (), jnp.float32),
    }


def reference(gated, value, upstream, residue, rate, skip_weight):
    length = TOKENS
    block_size = math.gcd(D, 64)
    block_count = D // block_size

    def per_block(items):
        gated_b, value_b, upstream_b, res_b, rate_b, skip_b = items
        positions = jnp.arange(length).astype(jnp.float32)
        basis = jnp.exp(-rate_b[:, :, None] * positions[None, None, :])
        filter_taps = jnp.einsum('cm,cml->cl', res_b, basis, precision=lax.Precision.HIGHEST)
        gated_f = gated_b.astype(jnp.float32)
        padded = 2 * length
        spec_g = jnp.fft.rfft(gated_f, n=padded, axis=1)
        spec_h = jnp.fft.rfft(filter_taps, n=padded, axis=1)
        conv = jnp.fft.irfft(spec_h * spec_g, n=padded, axis=1)[:, :length]
        forward_out = (conv + skip_b[:, None] * gated_f).astype(jnp.bfloat16)
        forward_out = lax.optimization_barrier(forward_out)
        grad_val = (upstream_b.astype(jnp.float32) * forward_out.astype(jnp.float32)).astype(jnp.bfloat16)
        grad_out = (upstream_b.astype(jnp.float32) * value_b.astype(jnp.float32)).astype(jnp.bfloat16)
        grad_f = lax.optimization_barrier(grad_out).astype(jnp.float32)
        spec_z = jnp.fft.rfft(grad_f, n=padded, axis=1)
        back = jnp.fft.irfft(jnp.conj(spec_h) * spec_z, n=padded, axis=1)[:, :length]
        grad_g = (back + skip_b[:, None] * grad_f).astype(jnp.bfloat16)
        dfilter = jnp.fft.irfft(jnp.conj(spec_g) * spec_z, n=padded, axis=1)[:, :length]
        grad_res = jnp.einsum('cl,cml->cm', dfilter, basis, precision=lax.Precision.HIGHEST) / length
        return grad_g, grad_val, grad_res

    items = (gated.reshape(block_count, block_size, length),
             value.reshape(block_count, block_size, length),
             upstream.reshape(block_count, block_size, length),
             residue.reshape(block_count, block_size, M),
             rate.reshape(block_count, block_size, M),
             skip_weight.reshape(block_count, block_size))
    grad_g, grad_val, grad_res = lax.map(per_block, items)
    return (grad_g.reshape(D, length), grad_val.reshape(D, length), grad_res.reshape(D, M))
```

```python
import functools

import jax
import jax.numpy as jnp
from jax import lax
from jax.experimental import pallas as pl
from jax.experimental.pallas import tpu as pltpu
from jax.sharding import PartitionSpec as P

F32 = jnp.float32
BF16 = jnp.bfloat16
LANES = 128
GROUP = 8
PART, UNROLL = 8, 16
LIMIT = 56 * 2**20


def transposed(block):
    return block.astype(F32).T


def spread_modes(src_ref, dst_ref, first, modes, blocks):
    for b in range(blocks):
        start = pl.multiple_of(first + b * LANES, LANES)
        dst_ref[pl.ds(b, modes, stride=blocks), :] = src_ref[:, pl.ds(start, LANES)]


def load_signals(gated_ref, value_ref, upstream_ref, gt, dzt, which, blocks, tokens):
    for b in which:
        rows = pl.ds(b * LANES, LANES)
        dz = upstream_ref[rows, :].astype(F32) * value_ref[rows, :].astype(F32)
        gt[pl.ds(b, tokens, stride=blocks), :] = transposed(gated_ref[rows, :])
        dzt[pl.ds(b, tokens, stride=blocks), :] = transposed(dz.astype(BF16))


def rows_of(ref, index, blocks, g):
    return ref[pl.ds(pl.multiple_of(index * blocks + g * GROUP, GROUP), GROUP), :]


def state_kernel(
    modes, blocks, tokens, gated_hbm, value_hbm, upstream_hbm, rate_hbm, out_ref,
    gated_ref, value_ref, upstream_ref, rate_ref, gt, dzt, lam, pack, sems
):
    half = GROUP * LANES
    groups = blocks // GROUP
    start = pl.multiple_of(lax.axis_index("ch") * (blocks * LANES), LANES)
    rate_copy = pltpu.make_async_copy(
        rate_hbm.at[:, pl.ds(start, blocks * LANES)], rate_ref, sems.at[3 * groups]
    )
    copies = []
    for g in range(groups):
        rows = pl.ds(g * half, half)
        pairs = ((gated_hbm, gated_ref), (upstream_hbm, upstream_ref), (value_hbm, value_ref))
        copies.append(
            [
                pltpu.make_async_copy(src.at[rows, :], dst.at[rows, :], sems.at[3 * g + k])
                for k, (src, dst) in enumerate(pairs)
            ]
        )
    for copy in copies[0] + [rate_copy] + [copy for part in copies[1:] for copy in part]:
        copy.start()
    unroll = UNROLL
    zero = jnp.zeros((GROUP, LANES), F32)
    for g in range(groups):
        for copy in copies[g]:
            copy.wait()
        which = range(g * GROUP, (g + 1) * GROUP)
        load_signals(gated_ref, value_ref, upstream_ref, gt, dzt, which, blocks, tokens)
        if g == 0:
            rate_copy.wait()
            spread_modes(rate_ref, lam, 0, modes, blocks)
        for m0 in range(0, modes, PART):
            decay = [jnp.exp(-rows_of(lam, m, blocks, g)) for m in range(m0, m0 + PART)]

            def body(i, carry, g=g, decay=decay):
                x, y, own = carry
                for u in range(unroll):
                    t = i * unroll + u
                    gv = rows_of(gt, t, blocks, g)
                    dv = rows_of(dzt, t, blocks, g)
                    rv = rows_of(dzt, tokens - 1 - t, blocks, g)
                    x = [a * v + gv for a, v in zip(decay, x)]
                    own = [o + dv * v for o, v in zip(own, x)]
                    y = [a * v + rv for a, v in zip(decay, y)]
                return x, y, own

            zeros = [zero] * PART
            x, y, own = lax.fori_loop(0, tokens // unroll, body, (zeros, zeros, zeros))
            for k in range(PART):
                base = ((m0 + k) * blocks + g * GROUP) * 4
                high = own[k].astype(BF16).astype(F32)
                for kind, rows in enumerate((x[k], y[k], high, own[k] - high)):
                    pack[pl.ds(base + kind, GROUP, stride=4), :] = rows
    out_ref[...] = pack[...].astype(BF16)


def rate_kernel(modes, blocks, rate_ref, lam_ref, lam):
    spread_modes(rate_ref, lam, lax.axis_index("ch") * (blocks * LANES), modes, blocks)
    for h in range(2):
        own = lam[pl.ds(lax.axis_index("seq") * 2 + h, 1), :]
        lam_ref[pl.ds(4 * h, 4), :] = jnp.broadcast_to(own, (4, LANES))


def own_kernel(
    modes, blocks, tokens, gated_ref, value_ref, upstream_ref, rate_ref, res_ref, skip_ref,
    fwd_ref, bwd_ref, dec_ref, gain_ref, gt, dzt
):
    first = lax.axis_index("ch") * (blocks * LANES)
    spread_modes(rate_ref, dec_ref, first, modes, blocks)
    spread_modes(res_ref, gain_ref, first, modes, blocks)
    load_signals(gated_ref, value_ref, upstream_ref, gt, dzt, range(blocks), blocks, tokens)
    dec_ref[...] = jnp.exp(-dec_ref[...])
    part, unroll = PART, UNROLL
    zero = jnp.zeros((GROUP, LANES), F32)
    for g in range(blocks // GROUP):
        skip = jnp.concatenate(
            [
                skip_ref[:, pl.ds(pl.multiple_of(first + (g * GROUP + j) * LANES, LANES), LANES)]
                for j in range(GROUP)
            ],
            axis=0,
        )
        for m0 in range(0, modes, part):
            decay = [rows_of(dec_ref, m, blocks, g) for m in range(m0, m0 + part)]
            gain = [rows_of(gain_ref, m, blocks, g) for m in range(m0, m0 + part)]

            def body(i, carry, g=g, m0=m0, decay=decay, gain=gain, skip=skip):
                x, y = carry
                for u in range(unroll):
                    t = i * unroll + u
                    s = tokens - 1 - t
                    gv = rows_of(gt, t, blocks, g)
                    dv = rows_of(dzt, s, blocks, g)
                    x = [a * v + gv for a, v in zip(decay, x)]
                    y = [a * v + dv for a, v in zip(decay, y)]
                    fwd = rows_of(fwd_ref, t, blocks, g) if m0 else skip * gv
                    bwd = rows_of(bwd_ref, s, blocks, g) if m0 else skip * dv
                    fwd = total([r * v for r, v in zip(gain, x)] + [fwd])
                    bwd = total([r * v for r, v in zip(gain, y)] + [bwd])
                    fwd_ref[pl.ds(pl.multiple_of(t * blocks + g * GROUP, GROUP), GROUP), :] = fwd
                    bwd_ref[pl.ds(pl.multiple_of(s * blocks + g * GROUP, GROUP), GROUP), :] = bwd
                return x, y

            zeros = [zero] * part
            lax.fori_loop(0, tokens // unroll, body, (zeros, zeros))


def total(terms):
    while len(terms) > 1:
        pairs = [a + b for a, b in zip(terms[::2], terms[1::2])]
        terms = pairs + ([terms[-1]] if len(terms) % 2 else [])
    return terms[0]


def scan_kernel(chunks, tokens, in_ref, lam_ref, out_ref, tiles, ahead, behind):
    tiles[...] = in_ref[...].astype(F32)
    lam = lam_ref[...]
    step = jnp.exp(lam * (-1.0 * tokens))
    kind = lax.broadcasted_iota(jnp.int32, (GROUP, LANES), 0) % 4
    unroll = 8
    zero = jnp.zeros((GROUP, LANES), F32)

    def tile_at(d):
        return pl.ds(pl.multiple_of(d * GROUP, GROUP), GROUP)

    def body(i, carry):
        fwd, bwd, own, cross = carry
        for u in range(unroll):
            d = i * unroll + u
            e = chunks - 1 - d
            here, there = tiles[tile_at(d), :], tiles[tile_at(e), :]
            ahead[tile_at(d), :] = fwd
            behind[tile_at(e), :] = bwd
            own = own + here
            cross = cross + here * pltpu.roll(fwd, 1, 0)
            fwd = step * fwd + here
            bwd = step * bwd + there
        return fwd, bwd, own, cross

    _, _, own, cross = lax.fori_loop(0, chunks // unroll, body, (zero, zero, zero, zero))
    cross = cross * jnp.exp(-lam)
    grad = own + pltpu.roll(own, GROUP - 1, 0) + pltpu.roll(cross, 1, 0)
    grad = grad * (1.0 / (chunks * tokens))
    high = grad.astype(BF16).astype(F32)
    tail = jnp.where(kind == 2, high, pltpu.roll(grad - high, 1, 0))

    def finish(i, carry):
        for u in range(unroll // 2):
            two = []
            for h in range(2):
                rows = tile_at((i * (unroll // 2) + u) * 2 + h)
                two.append(
                    jnp.where(kind == 0, ahead[rows, :], jnp.where(kind == 1, behind[rows, :], tail))
                )
            start = pl.multiple_of((i * (unroll // 2) + u) * 2 * GROUP, 2 * GROUP)
            out_ref[pl.ds(start, 2 * GROUP), :] = jnp.concatenate(two, axis=0).astype(BF16)
        return carry

    lax.fori_loop(0, chunks // unroll, finish, 0)


def residue_kernel(modes, blocks, in_ref, out_ref, tiles, flat):
    tiles[...] = in_ref[...].astype(F32)
    for r in range(modes * blocks // GROUP):
        base = r * GROUP * 4
        flat[pl.ds(r * GROUP, GROUP), :] = (
            tiles[pl.ds(base + 2, GROUP, stride=4), :] + tiles[pl.ds(base + 3, GROUP, stride=4), :]
        )
    for b in range(blocks):
        out_ref[:, pl.ds(b * LANES, LANES)] = flat[pl.ds(b, modes, stride=blocks), :]


def final_kernel(
    modes, blocks, tokens, in_ref, fwd_ref, bwd_ref, dec_ref, gain_ref, upstream_ref,
    grad_gated_hbm, grad_value_hbm, tiles, zt, gt, grad_gated_ref, grad_value_ref, sems
):
    tiles[...] = in_ref[...].astype(F32)
    unroll = UNROLL
    copies = []
    for g in range(blocks // GROUP):
        decay = [rows_of(dec_ref, m, blocks, g) for m in range(modes)]
        ahead, behind = [], []
        for m in range(modes):
            base = (m * blocks + g * GROUP) * 4
            scale = rows_of(gain_ref, m, blocks, g) * decay[m]
            ahead.append(tiles[pl.ds(base, GROUP, stride=4), :] * scale)
            behind.append(tiles[pl.ds(base + 1, GROUP, stride=4), :] * scale)

        def body(i, carry, g=g, decay=decay):
            x, y = carry
            for u in range(unroll):
                t = i * unroll + u
                s = tokens - 1 - t
                rows_t = pl.ds(pl.multiple_of(t * blocks + g * GROUP, GROUP), GROUP)
                rows_s = pl.ds(pl.multiple_of(s * blocks + g * GROUP, GROUP), GROUP)
                zt[rows_t, :] = fwd_ref[rows_t, :] + total(list(x))
                gt[rows_s, :] = bwd_ref[rows_s, :] + total(list(y))
                x = [a * v for a, v in zip(decay, x)]
                y = [a * v for a, v in zip(decay, y)]
            return x, y

        lax.fori_loop(0, tokens // unroll, body, (ahead, behind))
        for b in range(g * GROUP, (g + 1) * GROUP):
            rows = pl.ds(b * LANES, LANES)
            z = transposed(zt[pl.ds(b, tokens, stride=blocks), :].astype(BF16))
            grad_value_ref[rows, :] = (upstream_ref[rows, :].astype(F32) * z).astype(BF16)
            back = transposed(gt[pl.ds(b, tokens, stride=blocks), :].astype(BF16))
            grad_gated_ref[rows, :] = back.astype(BF16)
        rows = pl.ds(g * GROUP * LANES, GROUP * LANES)
        pairs = ((grad_gated_ref, grad_gated_hbm), (grad_value_ref, grad_value_hbm))
        for k, (src, dst) in enumerate(pairs):
            copy = pltpu.make_async_copy(src.at[rows, :], dst.at[rows, :], sems.at[2 * g + k])
            copy.start()
            copies.append(copy)
    for copy in copies:
        copy.wait()


def local(gated, value, upstream, residue, rate, skip_weight):
    channels, tokens = gated.shape
    modes = rate.shape[1]
    chunks = lax.axis_size("seq")
    blocks = channels // LANES
    pairs = modes * blocks
    assert tokens == LANES and pairs == 2 * chunks and blocks % GROUP == 0 and modes % 8 == 0
    rate_t, residue_t, skip = rate.T, residue.T, skip_weight[None, :]
    vmem = pl.BlockSpec(memory_space=pltpu.VMEM)
    hbm = pl.BlockSpec(memory_space=pltpu.HBM)
    cells = modes * channels * tokens

    def call(kernel, specs, out_specs, shapes, scratch, sems, flops, size, limit=16 * 2**20):
        return pl.pallas_call(
            kernel,
            in_specs=specs,
            out_specs=out_specs,
            out_shape=[jax.ShapeDtypeStruct(*shape) for shape in shapes],
            scratch_shapes=[pltpu.VMEM(*shape) for shape in scratch]
            + ([pltpu.SemaphoreType.DMA((sems,))] if sems else []),
            compiler_params=pltpu.CompilerParams(vmem_limit_bytes=limit),
            cost_estimate=pl.CostEstimate(flops=flops, bytes_accessed=size, transcendentals=0),
        )

    native = ((channels, tokens), BF16)
    signal = ((tokens * blocks, LANES), F32)
    per_mode = ((pairs, LANES), F32)
    wire = (chunks * GROUP, LANES)
    (states,) = call(
        functools.partial(state_kernel, modes, blocks, tokens),
        [hbm] * 4,
        [vmem],
        [(wire, BF16)],
        [native, native, native, ((modes, channels), F32), signal, signal, per_mode, (wire, F32)],
        3 * (blocks // GROUP) + 1,
        6 * cells,
        6 * channels * tokens,
        LIMIT,
    )(gated, value, upstream, rate_t)

    def exchange(array):
        array = array.reshape(chunks, GROUP, LANES)
        return lax.all_to_all(array, "seq", split_axis=0, concat_axis=0, tiled=True).reshape(wire)

    states, rate_held = lax.optimization_barrier((states, rate_t))
    (lam,) = call(
        functools.partial(rate_kernel, modes, blocks),
        [vmem],
        [vmem],
        [((GROUP, LANES), F32)],
        [per_mode],
        0,
        modes * channels,
        4 * modes * channels,
    )(rate_held)
    (entering,) = call(
        functools.partial(scan_kernel, chunks, tokens),
        [vmem] * 2,
        [vmem],
        [(wire, BF16)],
        [(wire, F32)] * 3,
        0,
        8 * chunks * GROUP * LANES,
        4 * chunks * GROUP * LANES,
    )(exchange(states), lam)
    entering, gated_held = lax.optimization_barrier((entering, gated))
    fwd, bwd, decay, gain = call(
        functools.partial(own_kernel, modes, blocks, tokens),
        [vmem] * 6,
        [vmem] * 4,
        [signal, signal, per_mode, per_mode],
        [signal, signal],
        0,
        8 * cells,
        14 * channels * tokens,
    )(gated_held, value, upstream, rate_t, residue_t, skip)
    returned, fwd, bwd = lax.optimization_barrier((exchange(entering), fwd, bwd))
    (grad_own,) = call(
        functools.partial(residue_kernel, modes, blocks),
        [vmem],
        [vmem],
        [((modes, channels), F32)],
        [(wire, F32), per_mode],
        0,
        modes * channels,
        8 * modes * channels,
    )(returned)
    grad_other = lax.ppermute(grad_own, "ch", [(0, 1), (1, 0)])
    grad_gated, grad_value = call(
        functools.partial(final_kernel, modes, blocks, tokens),
        [vmem] * 6,
        [hbm] * 2,
        [native, native],
        [(wire, F32), signal, signal, native, native],
        2 * (blocks // GROUP),
        4 * cells,
        14 * channels * tokens,
    )(returned, fwd, bwd, decay, gain, upstream)
    low = lax.axis_index("ch") == 0
    grad_res = jnp.concatenate(
        [jnp.where(low, grad_own, grad_other), jnp.where(low, grad_other, grad_own)], axis=1
    )
    return (grad_gated, grad_value, grad_res.T)


def solution(mesh):
    return jax.shard_map(
        local,
        mesh=mesh,
        in_specs=(P("ch", "seq"), P("ch", "seq"), P("ch", "seq"), P(), P(), P()),
        out_specs=(P("ch", "seq"), P("ch", "seq"), P()),
        check_vma=False,
    )
```

```python
import functools

import jax
import jax.numpy as jnp
from jax import lax
from jax.experimental import pallas as pl
from jax.experimental.pallas import tpu as pltpu
from jax.sharding import PartitionSpec as P

F32 = jnp.float32
BF16 = jnp.bfloat16
LANES = 128
GROUP = 8
PART, UNROLL = 8, 16
FINAL_UNROLL = 16
STATE_PART, STATE_UNROLL, RUN = 4, 32, 4
LIMIT = 56 * 2**20


def transposed(block):
    return block.astype(F32).T


def spread_modes(src_ref, dst_ref, first, modes, blocks):
    for b in range(blocks):
        start = pl.multiple_of(first + b * LANES, LANES)
        row = b // GROUP * modes * GROUP + b % GROUP
        dst_ref[pl.ds(row, modes, stride=GROUP), :] = src_ref[:, pl.ds(start, LANES)]


def tile(index):
    return pl.ds(pl.multiple_of(index * GROUP, GROUP), GROUP)


def put_signal(signal_ref, gt, b, j, tokens):
    gt[pl.ds(j, tokens, stride=GROUP), :] = transposed(signal_ref[pl.ds(b * LANES, LANES), :])


def put_dz(value_ref, upstream_ref, dz_ref, dzt, b, j, tokens):
    rows = pl.ds(b * LANES, LANES)
    dz = (upstream_ref[rows, :].astype(F32) * value_ref[rows, :].astype(F32)).astype(BF16)
    dz_ref[rows, :] = dz
    dzt[pl.ds(j, tokens, stride=GROUP), :] = transposed(dz)


def total(terms):
    while len(terms) > 1:
        pairs = [a + b for a, b in zip(terms[::2], terms[1::2])]
        terms = pairs + ([terms[-1]] if len(terms) % 2 else [])
    return terms[0]


def power(base, exponent):
    result = base
    for _ in range(exponent - 1):
        result = result * base
    return result


def horner(base, terms):
    result = terms[0]
    for term in terms[1:]:
        result = result * base + term
    return result


def state_kernel(
    modes, blocks, tokens, gated_hbm, value_hbm, upstream_hbm, rate_hbm, out_hbm, dz_hbm,
    gated_ref, value_ref, upstream_ref, dz_ref, rate_ref, gts, dzts, lam, pack, stage, sems, out_sems, dz_sems
):
    half = GROUP * LANES
    groups = blocks // GROUP
    start = pl.multiple_of(lax.axis_index("ch") * (blocks * LANES), LANES)
    rate_copy = pltpu.make_async_copy(
        rate_hbm.at[:, pl.ds(start, blocks * LANES)], rate_ref, sems.at[3 * groups]
    )
    copies = []
    for g in range(groups):
        rows = pl.ds(g * half, half)
        pairs = ((gated_hbm, gated_ref), (upstream_hbm, upstream_ref), (value_hbm, value_ref))
        copies.append(
            [
                pltpu.make_async_copy(src.at[rows, :], dst.at[rows, :], sems.at[3 * g + k])
                for k, (src, dst) in enumerate(pairs)
            ]
        )
    for copy in copies[0] + [rate_copy] + [copy for part in copies[1:] for copy in part]:
        copy.start()
    copies[0][0].wait()
    for j in range(GROUP):
        put_signal(gated_ref, gts[0], j, j, tokens)
    copies[0][1].wait()
    copies[0][2].wait()
    for j in range(GROUP):
        put_dz(value_ref, upstream_ref, dz_ref, dzts[0], j, j, tokens)
    rate_copy.wait()
    spread_modes(rate_ref, lam, 0, modes, blocks)
    zero = jnp.zeros((GROUP, LANES), F32)
    sent, late = [], []
    for g in range(groups):
        gt, dzt = gts[g], dzts[g]
        if g:
            for copy in copies[g]:
                copy.wait()
            for j in range(GROUP):
                put_signal(gated_ref, gt, g * GROUP + j, j, tokens)
                put_dz(value_ref, upstream_ref, dz_ref, dzt, g * GROUP + j, j, tokens)
        rows = pl.ds(g * half, half)
        copy = pltpu.make_async_copy(dz_ref.at[rows, :], dz_hbm.at[rows, :], dz_sems.at[g])
        copy.start()
        late.append(copy)
        lags = None
        for m0 in range(0, modes, STATE_PART):
            some = range(m0, m0 + STATE_PART)
            decay = [jnp.exp(-lam[tile(g * modes + m), :]) for m in some]
            jump = [power(a, RUN) for a in decay]

            def body(i, carry, gt=gt, dzt=dzt, decay=decay, jump=jump, first=m0 == 0):
                x, y, own, reach, lags = carry
                for u in range(STATE_UNROLL // RUN):
                    t = i * STATE_UNROLL + u * RUN
                    gs = [gt[tile(t + k), :] for k in range(RUN)]
                    ds = [dzt[tile(t + k), :] for k in range(RUN)]
                    if first:
                        lags = [
                            c + total([d * v for d, v in zip(ds[k:], gs)])
                            for k, c in enumerate(lags)
                        ]
                    ends = [horner(a, gs) for a in decay]
                    starts = [horner(a, ds[::-1]) for a in decay]
                    own = [o + v * w for o, v, w in zip(own, x, starts)]
                    y = [v + p * w for v, p, w in zip(y, reach, starts)]
                    x = [a * v + w for a, v, w in zip(jump, x, ends)]
                    reach = [a * p for a, p in zip(jump, reach)]
                return x, y, own, reach, lags

            zeros = [zero] * STATE_PART
            ones = [zero + 1.0] * STATE_PART
            carry = (zeros, zeros, zeros, ones, [zero] * RUN if m0 == 0 else [])
            x, y, own, _, found = lax.fori_loop(0, tokens // STATE_UNROLL, body, carry)
            lags = found if m0 == 0 else lags
            for k in range(STATE_PART):
                base = (g * modes + m0 + k) * GROUP * 4
                term = decay[k] * own[k] + horner(decay[k], lags[::-1])
                high = term.astype(BF16).astype(F32)
                for kind, rows in enumerate((x[k], y[k], high, term - high)):
                    pack[pl.ds(base + kind, GROUP, stride=4), :] = rows
            rows = pl.ds((g * modes + m0) * GROUP * 4, STATE_PART * GROUP * 4)
            stage[rows, :] = pack[rows, :].astype(BF16)
            copy = pltpu.make_async_copy(
                stage.at[rows, :], out_hbm.at[rows, :], out_sems.at[len(sent)]
            )
            copy.start()
            sent.append(copy)
    for copy in sent + late:
        copy.wait()


def own_sums(modes, tokens, g, signal, out_ref, dec_ref, gain_ref, skip, order):
    zero = jnp.zeros((GROUP, LANES), F32)
    for m0 in range(0, modes, PART):
        decay = [dec_ref[tile(g * modes + m), :] for m in range(m0, m0 + PART)]
        gain = [gain_ref[tile(g * modes + m), :] for m in range(m0, m0 + PART)]

        def body(i, x, m0=m0, decay=decay, gain=gain):
            for u in range(UNROLL):
                t = order(i * UNROLL + u)
                at = tile(g * tokens + t)
                v = signal[tile(t), :]
                x = [a * w + v for a, w in zip(decay, x)]
                known = out_ref[at, :] if m0 else skip * v
                out_ref[at, :] = total([r * w for r, w in zip(gain, x)] + [known])
            return x

        lax.fori_loop(0, tokens // UNROLL, body, [zero] * PART)


def skip_of(skip_ref, first, g):
    parts = [
        skip_ref[:, pl.ds(pl.multiple_of(first + (g * GROUP + j) * LANES, LANES), LANES)]
        for j in range(GROUP)
    ]
    return jnp.concatenate(parts, axis=0)


def ahead_kernel(
    modes, blocks, tokens, gated_ref, rate_ref, res_ref, skip_ref,
    fwd_ref, dec_ref, gain_ref, lam_ref, gt
):
    first = lax.axis_index("ch") * (blocks * LANES)
    spread_modes(rate_ref, dec_ref, first, modes, blocks)
    spread_modes(res_ref, gain_ref, first, modes, blocks)
    for h in range(2):
        own = dec_ref[pl.ds(lax.axis_index("seq") * 2 + h, 1), :]
        lam_ref[pl.ds(4 * h, 4), :] = jnp.broadcast_to(own, (4, LANES))
    dec_ref[...] = jnp.exp(-dec_ref[...])
    for g in range(blocks // GROUP):
        for j in range(GROUP):
            put_signal(gated_ref, gt, g * GROUP + j, j, tokens)
        skip = skip_of(skip_ref, first, g)
        own_sums(modes, tokens, g, gt, fwd_ref, dec_ref, gain_ref, skip, lambda t: t)


def behind_kernel(modes, blocks, tokens, dz_ref, dec_ref, gain_ref, skip_ref, bwd_ref, dzt):
    first = lax.axis_index("ch") * (blocks * LANES)
    for g in range(blocks // GROUP):
        for j in range(GROUP):
            put_signal(dz_ref, dzt, g * GROUP + j, j, tokens)
        skip = skip_of(skip_ref, first, g)
        order = lambda t: tokens - 1 - t
        own_sums(modes, tokens, g, dzt, bwd_ref, dec_ref, gain_ref, skip, order)


def scan_kernel(chunks, tokens, in_ref, lam_ref, out_hbm, tiles, ahead, behind, stage, sems):
    tiles[...] = in_ref[...].astype(F32)
    lam = lam_ref[...]
    step = jnp.exp(lam * (-1.0 * tokens))
    kind = lax.broadcasted_iota(jnp.int32, (GROUP, LANES), 0) % 4
    unroll = 8
    zero = jnp.zeros((GROUP, LANES), F32)

    def body(i, carry):
        fwd, bwd, own, cross = carry
        for u in range(unroll):
            d = i * unroll + u
            e = chunks - 1 - d
            here, there = tiles[tile(d), :], tiles[tile(e), :]
            ahead[tile(d), :] = fwd
            behind[tile(e), :] = bwd
            own = own + here
            cross = cross + here * pltpu.roll(fwd, 1, 0)
            fwd = step * fwd + here
            bwd = step * bwd + there
        return fwd, bwd, own, cross

    _, _, own, cross = lax.fori_loop(0, chunks // unroll, body, (zero, zero, zero, zero))
    cross = cross * jnp.exp(-lam)
    grad = own + pltpu.roll(own, GROUP - 1, 0) + pltpu.roll(cross, 1, 0)
    grad = grad * (1.0 / (chunks * tokens))
    high = grad.astype(BF16).astype(F32)
    tail = jnp.where(kind == 2, high, pltpu.roll(grad - high, 1, 0))
    quarter = chunks // 4
    sent = []
    for part in range(4):
        for pair in range(quarter // 2):
            d = part * quarter + 2 * pair
            both = [
                jnp.where(
                    kind == 0,
                    ahead[pl.ds(e * GROUP, GROUP), :],
                    jnp.where(kind == 1, behind[pl.ds(e * GROUP, GROUP), :], tail),
                )
                for e in (d, d + 1)
            ]
            stage[pl.ds(d * GROUP, 2 * GROUP), :] = jnp.concatenate(both, axis=0).astype(BF16)
        rows = pl.ds(part * quarter * GROUP, quarter * GROUP)
        copy = pltpu.make_async_copy(stage.at[rows, :], out_hbm.at[rows, :], sems.at[part])
        copy.start()
        sent.append(copy)
    for copy in sent:
        copy.wait()


def residue_kernel(modes, blocks, in_ref, out_ref, tiles, flat):
    tiles[...] = in_ref[...].astype(F32)
    for r in range(modes * blocks // GROUP):
        base = r * GROUP * 4
        flat[pl.ds(r * GROUP, GROUP), :] = (
            tiles[pl.ds(base + 2, GROUP, stride=4), :] + tiles[pl.ds(base + 3, GROUP, stride=4), :]
        )
    for b in range(blocks):
        row = b // GROUP * modes * GROUP + b % GROUP
        out_ref[:, pl.ds(b * LANES, LANES)] = flat[pl.ds(row, modes, stride=GROUP), :]


def final_kernel(
    modes, blocks, tokens, in_ref, fwd_ref, bwd_hbm, dec_ref, gain_ref, upstream_hbm,
    grad_gated_hbm, grad_value_hbm, tiles, zts, gts, bwd_ref, upstream_ref, grad_gated_ref,
    grad_value_ref, in_sems, sems
):
    groups = blocks // GROUP
    half = GROUP * LANES
    own_copies = []
    for g in range(groups):
        rows = pl.ds(g * tokens * GROUP, tokens * GROUP)
        own_copies.append(
            pltpu.make_async_copy(bwd_hbm.at[rows, :], bwd_ref.at[rows, :], in_sems.at[g])
        )
    upstream_copy = pltpu.make_async_copy(upstream_hbm, upstream_ref, in_sems.at[groups])
    for copy in [own_copies[0], upstream_copy] + own_copies[1:]:
        copy.start()
    tiles[...] = in_ref[...].astype(F32)
    copies = []

    def send(src, dst, first, size):
        rows = pl.ds(first * LANES, size * LANES)
        copy = pltpu.make_async_copy(src.at[rows, :], dst.at[rows, :], sems.at[len(copies)])
        copy.start()
        copies.append(copy)

    for g in range(groups):
        decay = [dec_ref[tile(g * modes + m), :] for m in range(modes)]
        scale = [gain_ref[tile(g * modes + m), :] * decay[m] for m in range(modes)]

        def entering(kind, g=g, scale=scale):
            return [
                tiles[pl.ds((g * modes + m) * GROUP * 4 + kind, GROUP, stride=4), :] * scale[m]
                for m in range(modes)
            ]

        def ahead(i, x, g=g, decay=decay):
            for u in range(FINAL_UNROLL):
                t = i * FINAL_UNROLL + u
                zts[g][tile(t), :] = fwd_ref[tile(g * tokens + t), :] + total(list(x))
                x = [a * v for a, v in zip(decay, x)]
            return x

        def behind(i, y, g=g, decay=decay):
            for u in range(FINAL_UNROLL):
                s = tokens - 1 - i * FINAL_UNROLL - u
                gts[g][tile(s), :] = bwd_ref[tile(g * tokens + s), :] + total(list(y))
                y = [a * v for a, v in zip(decay, y)]
            return y

        lax.fori_loop(0, tokens // FINAL_UNROLL, ahead, entering(0))
        if g == 0:
            upstream_copy.wait()
        for j in range(GROUP):
            rows = pl.ds(g * half + j * LANES, LANES)
            z = transposed(zts[g][pl.ds(j, tokens, stride=GROUP), :].astype(BF16))
            grad_value_ref[rows, :] = (upstream_ref[rows, :].astype(F32) * z).astype(BF16)
        send(grad_value_ref, grad_value_hbm, g * GROUP, GROUP)
        own_copies[g].wait()
        lax.fori_loop(0, tokens // FINAL_UNROLL, behind, entering(1))
        for j in range(GROUP):
            rows = pl.ds(g * half + j * LANES, LANES)
            back = transposed(gts[g][pl.ds(j, tokens, stride=GROUP), :].astype(BF16))
            grad_gated_ref[rows, :] = back.astype(BF16)
            if j % 4 == 3:
                send(grad_gated_ref, grad_gated_hbm, g * GROUP + j - 3, 4)
    for copy in copies:
        copy.wait()


def local(gated, value, upstream, residue, rate, skip_weight):
    channels, tokens = gated.shape
    modes = rate.shape[1]
    chunks = lax.axis_size("seq")
    blocks = channels // LANES
    pairs = modes * blocks
    groups = blocks // GROUP
    assert tokens == LANES == UNROLL * GROUP and pairs == 2 * chunks
    assert blocks % GROUP == 0 and modes == 2 * PART and chunks % 8 == 0
    rate_t, residue_t, skip = rate.T, residue.T, skip_weight[None, :]
    vmem = pl.BlockSpec(memory_space=pltpu.VMEM)
    hbm = pl.BlockSpec(memory_space=pltpu.HBM)
    cells = modes * channels * tokens

    def call(kernel, specs, out_specs, shapes, scratch, flops, size, limit=16 * 2**20):
        return pl.pallas_call(
            kernel,
            in_specs=specs,
            out_specs=out_specs,
            out_shape=[jax.ShapeDtypeStruct(*shape) for shape in shapes],
            scratch_shapes=scratch,
            compiler_params=pltpu.CompilerParams(vmem_limit_bytes=limit),
            cost_estimate=pl.CostEstimate(flops=flops, bytes_accessed=size, transcendentals=0),
        )

    native = ((channels, tokens), BF16)
    signal = ((tokens * blocks, LANES), F32)
    per_mode = ((pairs, LANES), F32)
    wire = (chunks * GROUP, LANES)
    one = pltpu.VMEM((tokens * GROUP, LANES), F32)
    raw = pltpu.VMEM(*native)
    unpacked = pltpu.VMEM(wire, F32)
    staged = pltpu.VMEM(wire, BF16)
    flat = pltpu.VMEM(*per_mode)
    sems = lambda count: pltpu.SemaphoreType.DMA((count,))
    states, dz = call(
        functools.partial(state_kernel, modes, blocks, tokens),
        [hbm] * 4,
        [hbm] * 2,
        [(wire, BF16), native],
        [raw, raw, raw, raw, pltpu.VMEM((modes, channels), F32), [one] * groups, [one] * groups]
        + [flat, unpacked, staged, sems(3 * groups + 1), sems(pairs // GROUP // STATE_PART)]
        + [sems(groups)],
        5 * cells,
        8 * channels * tokens,
        LIMIT,
    )(gated, value, upstream, rate_t)

    def exchange(array):
        array = array.reshape(chunks, GROUP, LANES)
        return lax.all_to_all(array, "seq", split_axis=0, concat_axis=0, tiled=True).reshape(wire)

    states, gated_held = lax.optimization_barrier((states, gated))
    fwd, decay, gain, lam = call(
        functools.partial(ahead_kernel, modes, blocks, tokens),
        [vmem] * 4,
        [vmem] * 4,
        [signal, per_mode, per_mode, ((GROUP, LANES), F32)],
        [one],
        4 * cells,
        6 * channels * tokens,
    )(gated_held, rate_t, residue_t, skip)
    (entering,) = call(
        functools.partial(scan_kernel, chunks, tokens),
        [vmem] * 2,
        [hbm],
        [(wire, BF16)],
        [unpacked, unpacked, unpacked, staged, sems(4)],
        8 * chunks * GROUP * LANES,
        4 * chunks * GROUP * LANES,
    )(exchange(states), lam)
    entering, dz_held = lax.optimization_barrier((entering, dz))
    (bwd,) = call(
        functools.partial(behind_kernel, modes, blocks, tokens),
        [vmem] * 4,
        [vmem],
        [signal],
        [one],
        4 * cells,
        6 * channels * tokens,
    )(dz_held, decay, gain, skip)
    returned, bwd = lax.optimization_barrier((exchange(entering), bwd))
    (grad_own,) = call(
        functools.partial(residue_kernel, modes, blocks),
        [vmem],
        [vmem],
        [((modes, channels), F32)],
        [unpacked, flat],
        modes * channels,
        8 * modes * channels,
    )(returned)
    grad_other = lax.ppermute(grad_own, "ch", [(0, 1), (1, 0)])
    grad_gated, grad_value = call(
        functools.partial(final_kernel, modes, blocks, tokens),
        [vmem, vmem, hbm, vmem, vmem, hbm],
        [hbm] * 2,
        [native, native],
        [unpacked, [one] * groups, [one] * groups, pltpu.VMEM(*signal), raw, raw, raw]
        + [sems(groups + 1), sems(3 * groups)],
        4 * cells,
        14 * channels * tokens,
    )(returned, fwd, bwd, decay, gain, upstream)
    low = lax.axis_index("ch") == 0
    grad_res = jnp.concatenate(
        [jnp.where(low, grad_own, grad_other), jnp.where(low, grad_other, grad_own)], axis=1
    )
    return (grad_gated, grad_value, grad_res.T)


def solution(mesh):
    return jax.shard_map(
        local,
        mesh=mesh,
        in_specs=(P("ch", "seq"), P("ch", "seq"), P("ch", "seq"), P(), P(), P()),
        out_specs=(P("ch", "seq"), P("ch", "seq"), P()),
        check_vma=False,
    )
```

```python
import functools

import jax
import jax.numpy as jnp
from jax import lax
from jax.experimental import pallas as pl
from jax.experimental.pallas import tpu as pltpu
from jax.sharding import PartitionSpec as P

F32 = jnp.float32
BF16 = jnp.bfloat16
LANES = 128
GROUP = 8
KINDS = 3
PART, UNROLL = 8, 16
FINAL_UNROLL = 16
SCAN_UNROLL = 4
STATE_PART, STATE_UNROLL, RUN = 4, 32, 4
LIMIT = 56 * 2**20


def transposed(block):
    return block.astype(F32).T


def spread_modes(src_ref, dst_ref, first, modes, blocks):
    for b in range(blocks):
        start = pl.multiple_of(first + b * LANES, LANES)
        row = b // GROUP * modes * GROUP + b % GROUP
        dst_ref[pl.ds(row, modes, stride=GROUP), :] = src_ref[:, pl.ds(start, LANES)]


def tile(index):
    return pl.ds(pl.multiple_of(index * GROUP, GROUP), GROUP)


def put_signal(signal_ref, gt, b, j, tokens):
    gt[pl.ds(j, tokens, stride=GROUP), :] = transposed(signal_ref[pl.ds(b * LANES, LANES), :])


def put_dz(value_ref, upstream_ref, dz_ref, dzt, b, j, tokens):
    rows = pl.ds(b * LANES, LANES)
    dz = (upstream_ref[rows, :].astype(F32) * value_ref[rows, :].astype(F32)).astype(BF16)
    dz_ref[rows, :] = dz
    dzt[pl.ds(j, tokens, stride=GROUP), :] = transposed(dz)


def total(terms):
    while len(terms) > 1:
        pairs = [a + b for a, b in zip(terms[::2], terms[1::2])]
        terms = pairs + ([terms[-1]] if len(terms) % 2 else [])
    return terms[0]


def power(base, exponent):
    result = base
    for _ in range(exponent - 1):
        result = result * base
    return result


def horner(base, terms):
    result = terms[0]
    for term in terms[1:]:
        result = result * base + term
    return result


def state_kernel(
    modes, blocks, tokens, gated_hbm, value_hbm, upstream_hbm, rate_hbm, out_hbm, dz_hbm,
    gated_ref, value_ref, upstream_ref, dz_ref, rate_ref, gts, dzts, lam, pack, stage, sems, out_sems, dz_sems
):
    half = GROUP * LANES
    groups = blocks // GROUP
    start = pl.multiple_of(lax.axis_index("ch") * (blocks * LANES), LANES)
    rate_copy = pltpu.make_async_copy(
        rate_hbm.at[:, pl.ds(start, blocks * LANES)], rate_ref, sems.at[3 * groups]
    )
    copies = []
    for g in range(groups):
        rows = pl.ds(g * half, half)
        pairs = ((gated_hbm, gated_ref), (upstream_hbm, upstream_ref), (value_hbm, value_ref))
        copies.append(
            [
                pltpu.make_async_copy(src.at[rows, :], dst.at[rows, :], sems.at[3 * g + k])
                for k, (src, dst) in enumerate(pairs)
            ]
        )
    for copy in copies[0] + [rate_copy]:
        copy.start()
    copies[0][0].wait()
    for j in range(GROUP):
        put_signal(gated_ref, gts[0], j, j, tokens)
    copies[0][1].wait()
    copies[0][2].wait()
    for j in range(GROUP):
        put_dz(value_ref, upstream_ref, dz_ref, dzts[0], j, j, tokens)
    for part in copies[1:]:
        for copy in part:
            copy.start()
    rate_copy.wait()
    spread_modes(rate_ref, lam, 0, modes, blocks)
    zero = jnp.zeros((GROUP, LANES), F32)
    sent, late = [], []
    for g in range(groups):
        gt, dzt = gts[g], dzts[g]
        if g:
            for copy in copies[g]:
                copy.wait()
            for j in range(GROUP):
                put_signal(gated_ref, gt, g * GROUP + j, j, tokens)
                put_dz(value_ref, upstream_ref, dz_ref, dzt, g * GROUP + j, j, tokens)
        rows = pl.ds(g * half, half)
        copy = pltpu.make_async_copy(dz_ref.at[rows, :], dz_hbm.at[rows, :], dz_sems.at[g])
        copy.start()
        late.append(copy)
        lags = None
        for m0 in range(0, modes, STATE_PART):
            some = range(m0, m0 + STATE_PART)
            decay = [jnp.exp(-lam[tile(g * modes + m), :]) for m in some]
            jump = [power(a, RUN) for a in decay]

            def body(i, carry, gt=gt, dzt=dzt, decay=decay, jump=jump, first=m0 == 0):
                x, y, own, reach, lags = carry
                for u in range(STATE_UNROLL // RUN):
                    t = i * STATE_UNROLL + u * RUN
                    gs = [gt[tile(t + k), :] for k in range(RUN)]
                    ds = [dzt[tile(t + k), :] for k in range(RUN)]
                    if first:
                        lags = [
                            c + total([d * v for d, v in zip(ds[k:], gs)])
                            for k, c in enumerate(lags)
                        ]
                    ends = [horner(a, gs) for a in decay]
                    starts = [horner(a, ds[::-1]) for a in decay]
                    own = [o + v * w for o, v, w in zip(own, x, starts)]
                    y = [v + p * w for v, p, w in zip(y, reach, starts)]
                    x = [a * v + w for a, v, w in zip(jump, x, ends)]
                    reach = [a * p for a, p in zip(jump, reach)]
                return x, y, own, reach, lags

            zeros = [zero] * STATE_PART
            ones = [zero + 1.0] * STATE_PART
            carry = (zeros, zeros, zeros, ones, [zero] * RUN if m0 == 0 else [])
            x, y, own, _, found = lax.fori_loop(0, tokens // STATE_UNROLL, body, carry)
            lags = found if m0 == 0 else lags
            for k in range(STATE_PART):
                base = (m0 + k) * GROUP * 2 * KINDS + g * KINDS
                term = decay[k] * own[k] + horner(decay[k], lags[::-1])
                for kind, rows in enumerate((x[k], y[k], term)):
                    pack[pl.ds(base + kind, GROUP, stride=2 * KINDS), :] = rows
            if g < groups - 1:
                continue
            rows = pl.ds(m0 * GROUP * 2 * KINDS, STATE_PART * GROUP * 2 * KINDS)
            stage[rows, :] = pack[rows, :].astype(BF16)
            copy = pltpu.make_async_copy(
                stage.at[rows, :], out_hbm.at[rows, :], out_sems.at[len(sent)]
            )
            copy.start()
            sent.append(copy)
    for copy in sent + late:
        copy.wait()


def own_sums(modes, tokens, g, signal, out_ref, dec_ref, gain_ref, skip, order):
    zero = jnp.zeros((GROUP, LANES), F32)
    for m0 in range(0, modes, PART):
        decay = [dec_ref[tile(g * modes + m), :] for m in range(m0, m0 + PART)]
        gain = [gain_ref[tile(g * modes + m), :] for m in range(m0, m0 + PART)]

        def body(i, x, m0=m0, decay=decay, gain=gain):
            for u in range(UNROLL):
                t = order(i * UNROLL + u)
                at = tile(g * tokens + t)
                v = signal[tile(t), :]
                x = [a * w + v for a, w in zip(decay, x)]
                known = out_ref[at, :] if m0 else skip * v
                out_ref[at, :] = total([r * w for r, w in zip(gain, x)] + [known])
            return x

        lax.fori_loop(0, tokens // UNROLL, body, [zero] * PART)


def skip_of(skip_ref, first, g):
    parts = [
        skip_ref[:, pl.ds(pl.multiple_of(first + (g * GROUP + j) * LANES, LANES), LANES)]
        for j in range(GROUP)
    ]
    return jnp.concatenate(parts, axis=0)


def ahead_kernel(
    modes, blocks, tokens, gated_ref, rate_ref, res_ref, skip_ref,
    fwd_ref, dec_ref, gain_ref, lam_ref, gt
):
    first = lax.axis_index("ch") * (blocks * LANES)
    spread_modes(rate_ref, dec_ref, first, modes, blocks)
    spread_modes(res_ref, gain_ref, first, modes, blocks)
    for h in range(2):
        for g in range(blocks // GROUP):
            row = g * modes * GROUP + lax.axis_index("seq") // 2 * 2 + h
            own = dec_ref[pl.ds(row, 1), :]
            lam_ref[pl.ds(2 * h + g, 1), :] = own
    dec_ref[...] = jnp.exp(-dec_ref[...])
    for g in range(blocks // GROUP):
        for j in range(GROUP):
            put_signal(gated_ref, gt, g * GROUP + j, j, tokens)
        skip = skip_of(skip_ref, first, g)
        own_sums(modes, tokens, g, gt, fwd_ref, dec_ref, gain_ref, skip, lambda t: t)


def behind_kernel(modes, blocks, tokens, dz_ref, dec_ref, gain_ref, skip_ref, bwd_ref, dzt):
    first = lax.axis_index("ch") * (blocks * LANES)
    for g in range(blocks // GROUP):
        for j in range(GROUP):
            put_signal(dz_ref, dzt, g * GROUP + j, j, tokens)
        skip = skip_of(skip_ref, first, g)
        order = lambda t: tokens - 1 - t
        own_sums(modes, tokens, g, dzt, bwd_ref, dec_ref, gain_ref, skip, order)


def scan_kernel(chunks, tokens, own_ref, other_ref, lam_ref, out_hbm, sums, outs, stage, sems):
    core = lax.axis_index("seq") % 2
    chips = chunks // 2
    sums[core] = own_ref[...].astype(F32)
    sums[1 - core] = other_ref[...].astype(F32)
    lam = lam_ref[...]
    step = jnp.exp(lam * (-1.0 * tokens))
    zero = jnp.zeros((4, LANES), F32)

    def at(q, kind):
        return pl.ds(q * 4 * KINDS + kind, 4, stride=KINDS)

    def body(i, carry):
        x, y, own, cross = carry
        for u in range(SCAN_UNROLL):
            q, r = i * SCAN_UNROLL + u, chips - 1 - i * SCAN_UNROLL - u
            for place in range(2):
                outs[place, at(q, 0), :] = x
                outs[1 - place, at(r, 1), :] = y
                own = own + sums[place, at(q, 2), :]
                cross = cross + sums[place, at(q, 1), :] * x
                x = step * x + sums[place, at(q, 0), :]
                y = step * y + sums[1 - place, at(r, 1), :]
        return x, y, own, cross

    _, _, own, cross = lax.fori_loop(0, chips // SCAN_UNROLL, body, (zero, zero, zero, zero))
    grad = (own + cross * jnp.exp(-lam)) * (1.0 / (chunks * tokens))
    sent = []
    quarter = chips // 4
    for part in range(4):
        for q in range(part * quarter, (part + 1) * quarter):
            outs[core, at(q, 2), :] = grad
        rows = pl.ds(part * quarter * 4 * KINDS, quarter * 4 * KINDS)
        stage[rows, :] = outs[core, rows, :].astype(BF16)
        copy = pltpu.make_async_copy(stage.at[rows, :], out_hbm.at[rows, :], sems.at[part])
        copy.start()
        sent.append(copy)
    for copy in sent:
        copy.wait()


def residue_kernel(modes, blocks, in_ref, out_ref, wire_ref, tiles, flat):
    tiles[...] = in_ref[...].astype(F32)
    for r in range(modes * blocks // GROUP):
        base = r % modes * GROUP * 2 * KINDS + r // modes * KINDS
        flat[pl.ds(r * GROUP, GROUP), :] = tiles[pl.ds(base + 2, GROUP, stride=2 * KINDS), :]
    for b in range(blocks):
        row = b // GROUP * modes * GROUP + b % GROUP
        found = flat[pl.ds(row, modes, stride=GROUP), :]
        out_ref[:, pl.ds(b * LANES, LANES)] = found
        wire_ref[:, pl.ds(b * LANES, LANES)] = found.astype(BF16)


def final_kernel(
    modes, blocks, tokens, in_ref, fwd_ref, bwd_hbm, dec_ref, gain_ref, upstream_hbm,
    grad_gated_hbm, grad_value_hbm, tiles, zts, gts, bwd_ref, upstream_ref, grad_gated_ref,
    grad_value_ref, in_sems, sems
):
    groups = blocks // GROUP
    half = GROUP * LANES
    own_copies = []
    for g in range(groups):
        rows = pl.ds(g * tokens * GROUP, tokens * GROUP)
        own_copies.append(
            pltpu.make_async_copy(bwd_hbm.at[rows, :], bwd_ref.at[rows, :], in_sems.at[g])
        )
    upstream_copy = pltpu.make_async_copy(upstream_hbm, upstream_ref, in_sems.at[groups])
    for copy in [own_copies[0], upstream_copy] + own_copies[1:]:
        copy.start()
    tiles[...] = in_ref[...].astype(F32)
    copies = []

    def send(src, dst, first, size):
        rows = pl.ds(first * LANES, size * LANES)
        copy = pltpu.make_async_copy(src.at[rows, :], dst.at[rows, :], sems.at[len(copies)])
        copy.start()
        copies.append(copy)

    for g in range(groups):
        decay = [dec_ref[tile(g * modes + m), :] for m in range(modes)]
        scale = [gain_ref[tile(g * modes + m), :] * decay[m] for m in range(modes)]

        def entering(kind, g=g, scale=scale):
            bases = [m * GROUP * 2 * KINDS + g * KINDS + kind for m in range(modes)]
            return [
                tiles[pl.ds(base, GROUP, stride=2 * KINDS), :] * a for base, a in zip(bases, scale)
            ]

        def ahead(i, x, g=g, decay=decay):
            for u in range(FINAL_UNROLL):
                t = i * FINAL_UNROLL + u
                zts[g][tile(t), :] = fwd_ref[tile(g * tokens + t), :] + total(list(x))
                x = [a * v for a, v in zip(decay, x)]
            return x

        def behind(i, y, g=g, decay=decay):
            for u in range(FINAL_UNROLL):
                s = tokens - 1 - i * FINAL_UNROLL - u
                gts[g][tile(s), :] = bwd_ref[tile(g * tokens + s), :] + total(list(y))
                y = [a * v for a, v in zip(decay, y)]
            return y

        lax.fori_loop(0, tokens // FINAL_UNROLL, ahead, entering(0))
        if g == 0:
            upstream_copy.wait()
        for j in range(GROUP):
            rows = pl.ds(g * half + j * LANES, LANES)
            z = transposed(zts[g][pl.ds(j, tokens, stride=GROUP), :].astype(BF16))
            grad_value_ref[rows, :] = (upstream_ref[rows, :].astype(F32) * z).astype(BF16)
        send(grad_value_ref, grad_value_hbm, g * GROUP, GROUP)
        own_copies[g].wait()
        lax.fori_loop(0, tokens // FINAL_UNROLL, behind, entering(1))
        for j in range(GROUP):
            rows = pl.ds(g * half + j * LANES, LANES)
            back = transposed(gts[g][pl.ds(j, tokens, stride=GROUP), :].astype(BF16))
            grad_gated_ref[rows, :] = back.astype(BF16)
            if j % 4 == 3:
                send(grad_gated_ref, grad_gated_hbm, g * GROUP + j - 3, 4)
    for copy in copies:
        copy.wait()


def local(gated, value, upstream, residue, rate, skip_weight):
    channels, tokens = gated.shape
    modes = rate.shape[1]
    chunks = lax.axis_size("seq")
    blocks = channels // LANES
    pairs = modes * blocks
    groups = blocks // GROUP
    assert tokens == LANES == UNROLL * GROUP and pairs == 2 * chunks
    assert blocks == 2 * GROUP and modes == 2 * PART and chunks % (2 * SCAN_UNROLL) == 0
    rate_t, residue_t, skip = rate.T, residue.T, skip_weight[None, :]
    vmem = pl.BlockSpec(memory_space=pltpu.VMEM)
    hbm = pl.BlockSpec(memory_space=pltpu.HBM)
    cells = modes * channels * tokens

    def call(kernel, specs, out_specs, shapes, scratch, flops, size, limit=16 * 2**20):
        return pl.pallas_call(
            kernel,
            in_specs=specs,
            out_specs=out_specs,
            out_shape=[jax.ShapeDtypeStruct(*shape) for shape in shapes],
            scratch_shapes=scratch,
            compiler_params=pltpu.CompilerParams(vmem_limit_bytes=limit),
            cost_estimate=pl.CostEstimate(flops=flops, bytes_accessed=size, transcendentals=0),
        )

    native = ((channels, tokens), BF16)
    signal = ((tokens * blocks, LANES), F32)
    per_mode = ((pairs, LANES), F32)
    wire = (chunks * 2 * KINDS, LANES)
    one = pltpu.VMEM((tokens * GROUP, LANES), F32)
    raw = pltpu.VMEM(*native)
    unpacked = pltpu.VMEM(wire, F32)
    staged = pltpu.VMEM(wire, BF16)
    flat = pltpu.VMEM(*per_mode)
    sems = lambda count: pltpu.SemaphoreType.DMA((count,))
    states, dz = call(
        functools.partial(state_kernel, modes, blocks, tokens),
        [hbm] * 4,
        [hbm] * 2,
        [(wire, BF16), native],
        [raw, raw, raw, raw, pltpu.VMEM((modes, channels), F32), [one] * groups, [one] * groups]
        + [flat, unpacked, staged, sems(3 * groups + 1), sems(modes // STATE_PART)]
        + [sems(groups)],
        5 * cells,
        8 * channels * tokens,
        LIMIT,
    )(gated, value, upstream, rate_t)

    def exchange(array):
        array = array.reshape(chunks // 2, KINDS, 4, LANES)
        members = [list(range(core, chunks, 2)) for core in range(2)]
        return lax.all_to_all(
            array, "seq", split_axis=0, concat_axis=0, axis_index_groups=members, tiled=True
        ).reshape(wire)

    states, gated_held = lax.optimization_barrier((states, gated))
    fwd, decay, gain, lam = call(
        functools.partial(ahead_kernel, modes, blocks, tokens),
        [vmem] * 4,
        [vmem] * 4,
        [signal, per_mode, per_mode, ((4, LANES), F32)],
        [one],
        4 * cells,
        6 * channels * tokens,
    )(gated_held, rate_t, residue_t, skip)
    heard, fwd, lam = lax.optimization_barrier((exchange(states), fwd, lam))
    heard_other = lax.ppermute(heard, "seq", [(d, d ^ 1) for d in range(chunks)])
    chained = pltpu.VMEM((2,) + wire, F32)
    (entering,) = call(
        functools.partial(scan_kernel, chunks, tokens),
        [vmem] * 3,
        [hbm],
        [(wire, BF16)],
        [chained, chained, staged, sems(4)],
        16 * chunks * GROUP * LANES,
        8 * chunks * GROUP * LANES,
    )(heard, heard_other, lam)
    entering, dz_held = lax.optimization_barrier((entering, dz))
    (bwd,) = call(
        functools.partial(behind_kernel, modes, blocks, tokens),
        [vmem] * 4,
        [vmem],
        [signal],
        [one],
        4 * cells,
        6 * channels * tokens,
    )(dz_held, decay, gain, skip)
    returned, bwd = lax.optimization_barrier((exchange(entering), bwd))
    grad_own, grad_wire = call(
        functools.partial(residue_kernel, modes, blocks),
        [vmem],
        [vmem] * 2,
        [((modes, channels), F32), ((modes, channels), BF16)],
        [unpacked, flat],
        modes * channels,
        8 * modes * channels,
    )(returned)
    grad_other = lax.ppermute(grad_wire, "ch", [(0, 1), (1, 0)]).astype(F32)
    grad_gated, grad_value = call(
        functools.partial(final_kernel, modes, blocks, tokens),
        [vmem, vmem, hbm, vmem, vmem, hbm],
        [hbm] * 2,
        [native, native],
        [unpacked, [one] * groups, [one] * groups, pltpu.VMEM(*signal), raw, raw, raw]
        + [sems(groups + 1), sems(3 * groups)],
        4 * cells,
        14 * channels * tokens,
    )(returned, fwd, bwd, decay, gain, upstream)
    low = lax.axis_index("ch") == 0
    grad_res = jnp.concatenate(
        [jnp.where(low, grad_own, grad_other), jnp.where(low, grad_other, grad_own)], axis=1
    )
    return (grad_gated, grad_value, grad_res.T)


def solution(mesh):
    return jax.shard_map(
        local,
        mesh=mesh,
        in_specs=(P("ch", "seq"), P("ch", "seq"), P("ch", "seq"), P(), P(), P()),
        out_specs=(P("ch", "seq"), P("ch", "seq"), P()),
        check_vma=False,
    )
```

```python
import functools

import jax
import jax.numpy as jnp
from jax import lax
from jax.experimental import pallas as pl
from jax.experimental.pallas import tpu as pltpu
from jax.sharding import PartitionSpec as P

F32 = jnp.float32
BF16 = jnp.bfloat16
LANES = 128
GROUP = 8
KINDS = 3
PART, UNROLL = 8, 16
FINAL_UNROLL = 16
SCAN_UNROLL = 4
STATE_PART, STATE_UNROLL, RUN = 4, 32, 4
LIMIT = 56 * 2**20


def transposed(block):
    return block.astype(F32).T


def spread_modes(src_ref, dst_ref, first, modes, blocks):
    for b in range(blocks):
        start = pl.multiple_of(first + b * LANES, LANES)
        row = b // GROUP * modes * GROUP + b % GROUP
        dst_ref[pl.ds(row, modes, stride=GROUP), :] = src_ref[:, pl.ds(start, LANES)]


def tile(index):
    return pl.ds(pl.multiple_of(index * GROUP, GROUP), GROUP)


def put_signal(signal_ref, gt, b, j, tokens):
    gt[pl.ds(j, tokens, stride=GROUP), :] = transposed(signal_ref[pl.ds(b * LANES, LANES), :])


def put_dz(value_ref, upstream_ref, dz_ref, dzt, b, j, tokens):
    rows = pl.ds(b * LANES, LANES)
    dz = (upstream_ref[rows, :].astype(F32) * value_ref[rows, :].astype(F32)).astype(BF16)
    dz_ref[rows, :] = dz
    dzt[pl.ds(j, tokens, stride=GROUP), :] = transposed(dz)


def total(terms):
    while len(terms) > 1:
        pairs = [a + b for a, b in zip(terms[::2], terms[1::2])]
        terms = pairs + ([terms[-1]] if len(terms) % 2 else [])
    return terms[0]


def power(base, exponent):
    result = base
    for _ in range(exponent - 1):
        result = result * base
    return result


def horner(base, terms):
    result = terms[0]
    for term in terms[1:]:
        result = result * base + term
    return result


def state_kernel(
    modes, blocks, tokens, gated_hbm, value_hbm, upstream_hbm, rate_hbm, out_hbm, dz_hbm, edge_hbm,
    gated_ref, value_ref, upstream_ref, dz_ref, rate_ref, gts, dzts, lam, pack, stage, edge, sems, out_sems, dz_sems
):
    half = GROUP * LANES
    groups = blocks // GROUP
    start = pl.multiple_of(lax.axis_index("ch") * (blocks * LANES), LANES)
    rate_copy = pltpu.make_async_copy(
        rate_hbm.at[:, pl.ds(start, blocks * LANES)], rate_ref, sems.at[3 * groups]
    )
    copies = []
    for g in range(groups):
        rows = pl.ds(g * half, half)
        pairs = ((gated_hbm, gated_ref), (upstream_hbm, upstream_ref), (value_hbm, value_ref))
        copies.append(
            [
                pltpu.make_async_copy(src.at[rows, :], dst.at[rows, :], sems.at[3 * g + k])
                for k, (src, dst) in enumerate(pairs)
            ]
        )
    for copy in copies[0] + [rate_copy]:
        copy.start()
    copies[0][0].wait()
    for j in range(GROUP):
        put_signal(gated_ref, gts[0], j, j, tokens)
    copies[0][1].wait()
    copies[0][2].wait()
    for j in range(GROUP):
        put_dz(value_ref, upstream_ref, dz_ref, dzts[0], j, j, tokens)
    for part in copies[1:]:
        for copy in part:
            copy.start()
    rate_copy.wait()
    spread_modes(rate_ref, lam, 0, modes, blocks)
    zero = jnp.zeros((GROUP, LANES), F32)
    sent, late = [], []
    early = jnp.broadcast_to(lax.axis_index("seq") % 2, (GROUP, LANES)) == 0
    for g in range(groups):
        gt, dzt = gts[g], dzts[g]
        if g:
            for copy in copies[g]:
                copy.wait()
            for j in range(GROUP):
                put_signal(gated_ref, gt, g * GROUP + j, j, tokens)
                put_dz(value_ref, upstream_ref, dz_ref, dzt, g * GROUP + j, j, tokens)
        rows = pl.ds(g * half, half)
        copy = pltpu.make_async_copy(dz_ref.at[rows, :], dz_hbm.at[rows, :], dz_sems.at[g])
        copy.start()
        late.append(copy)
        lags = None
        for m0 in range(0, modes, STATE_PART):
            some = range(m0, m0 + STATE_PART)
            decay = [jnp.exp(-lam[tile(g * modes + m), :]) for m in some]
            jump = [power(a, RUN) for a in decay]

            def body(i, carry, gt=gt, dzt=dzt, decay=decay, jump=jump, first=m0 == 0):
                x, y, own, reach, lags = carry
                for u in range(STATE_UNROLL // RUN):
                    t = i * STATE_UNROLL + u * RUN
                    gs = [gt[tile(t + k), :] for k in range(RUN)]
                    ds = [dzt[tile(t + k), :] for k in range(RUN)]
                    if first:
                        lags = [
                            c + total([d * v for d, v in zip(ds[k:], gs)])
                            for k, c in enumerate(lags)
                        ]
                    ends = [horner(a, gs) for a in decay]
                    starts = [horner(a, ds[::-1]) for a in decay]
                    own = [o + v * w for o, v, w in zip(own, x, starts)]
                    y = [v + p * w for v, p, w in zip(y, reach, starts)]
                    x = [a * v + w for a, v, w in zip(jump, x, ends)]
                    reach = [a * p for a, p in zip(jump, reach)]
                return x, y, own, reach, lags

            zeros = [zero] * STATE_PART
            ones = [zero + 1.0] * STATE_PART
            carry = (zeros, zeros, zeros, ones, [zero] * RUN if m0 == 0 else [])
            x, y, own, _, found = lax.fori_loop(0, tokens // STATE_UNROLL, body, carry)
            lags = found if m0 == 0 else lags
            for k in range(STATE_PART):
                base = (m0 + k) * GROUP * 2 * KINDS + g * KINDS
                term = decay[k] * own[k] + horner(decay[k], lags[::-1])
                edge[tile(g * modes + m0 + k), :] = jnp.where(early, x[k], y[k])
                for kind, rows in enumerate((x[k], y[k], term)):
                    pack[pl.ds(base + kind, GROUP, stride=2 * KINDS), :] = rows
            if g < groups - 1:
                continue
            rows = pl.ds(m0 * GROUP * 2 * KINDS, STATE_PART * GROUP * 2 * KINDS)
            stage[rows, :] = pack[rows, :].astype(BF16)
            copy = pltpu.make_async_copy(
                stage.at[rows, :], out_hbm.at[rows, :], out_sems.at[len(sent)]
            )
            copy.start()
            sent.append(copy)
    copy = pltpu.make_async_copy(edge, edge_hbm, dz_sems.at[groups])
    copy.start()
    for copy in sent + late + [copy]:
        copy.wait()


def own_sums(modes, tokens, g, signal, out_ref, dec_ref, gain_ref, skip, order):
    zero = jnp.zeros((GROUP, LANES), F32)
    for m0 in range(0, modes, PART):
        decay = [dec_ref[tile(g * modes + m), :] for m in range(m0, m0 + PART)]
        gain = [gain_ref[tile(g * modes + m), :] for m in range(m0, m0 + PART)]

        def body(i, x, m0=m0, decay=decay, gain=gain):
            for u in range(UNROLL):
                t = order(i * UNROLL + u)
                at = tile(g * tokens + t)
                v = signal[tile(t), :]
                x = [a * w + v for a, w in zip(decay, x)]
                known = out_ref[at, :] if m0 else skip * v
                out_ref[at, :] = total([r * w for r, w in zip(gain, x)] + [known])
            return x

        lax.fori_loop(0, tokens // UNROLL, body, [zero] * PART)


def skip_of(skip_ref, first, g):
    parts = [
        skip_ref[:, pl.ds(pl.multiple_of(first + (g * GROUP + j) * LANES, LANES), LANES)]
        for j in range(GROUP)
    ]
    return jnp.concatenate(parts, axis=0)


def ahead_kernel(
    modes, blocks, tokens, gated_ref, rate_ref, res_ref, skip_ref,
    fwd_ref, dec_ref, gain_ref, lam_ref, gt
):
    first = lax.axis_index("ch") * (blocks * LANES)
    spread_modes(rate_ref, dec_ref, first, modes, blocks)
    spread_modes(res_ref, gain_ref, first, modes, blocks)
    for h in range(2):
        for g in range(blocks // GROUP):
            row = g * modes * GROUP + lax.axis_index("seq") // 2 * 2 + h
            own = dec_ref[pl.ds(row, 1), :]
            lam_ref[pl.ds(2 * h + g, 1), :] = own
    dec_ref[...] = jnp.exp(-dec_ref[...])
    for g in range(blocks // GROUP):
        for j in range(GROUP):
            put_signal(gated_ref, gt, g * GROUP + j, j, tokens)
        skip = skip_of(skip_ref, first, g)
        own_sums(modes, tokens, g, gt, fwd_ref, dec_ref, gain_ref, skip, lambda t: t)


def behind_kernel(modes, blocks, tokens, dz_ref, dec_ref, gain_ref, skip_ref, bwd_ref, dzt):
    first = lax.axis_index("ch") * (blocks * LANES)
    for g in range(blocks // GROUP):
        for j in range(GROUP):
            put_signal(dz_ref, dzt, g * GROUP + j, j, tokens)
        skip = skip_of(skip_ref, first, g)
        order = lambda t: tokens - 1 - t
        own_sums(modes, tokens, g, dzt, bwd_ref, dec_ref, gain_ref, skip, order)


def scan_kernel(chunks, tokens, own_ref, other_ref, lam_ref, out_ref, sums, outs, grads):
    core = lax.axis_index("seq") % 2
    chips = chunks // 2
    sums[core] = own_ref[...].astype(F32)
    sums[1 - core] = other_ref[...].astype(F32)
    lam = lam_ref[...]
    step = jnp.exp(lam * (-1.0 * tokens))
    zero = jnp.zeros((4, LANES), F32)

    def at(q, kind):
        return pl.ds(q * 4 * KINDS + kind, 4, stride=KINDS)

    def body(i, carry):
        x, y, own, cross = carry
        for u in range(SCAN_UNROLL):
            q, r = i * SCAN_UNROLL + u, chips - 1 - i * SCAN_UNROLL - u
            for h in range(2):
                outs[0, pl.ds(q * 6 + 3 * h, 2), :] = x[2 * h : 2 * h + 2]
                outs[1, pl.ds(r * 6 + 3 * h, 2), :] = y[2 * h : 2 * h + 2]
            for place in range(2):
                own = own + sums[place, at(q, 2), :]
                cross = cross + sums[place, at(q, 1), :] * x
                x = step * x + sums[place, at(q, 0), :]
                y = step * y + sums[1 - place, at(r, 1), :]
        return x, y, own, cross

    _, _, own, cross = lax.fori_loop(0, chips // SCAN_UNROLL, body, (zero, zero, zero, zero))
    grads[...] = (own + cross * jnp.exp(-lam)) * (1.0 / (chunks * tokens))
    grad = grads[pl.ds(core, 2, stride=2), :]
    for q in range(chips):
        outs[core, pl.ds(q * 6 + 2, 2, stride=3), :] = grad
    out_ref[...] = outs[core].astype(BF16)


def residue_kernel(modes, blocks, own_ref, other_ref, out_ref, wire_ref, tiles, flat):
    core = lax.axis_index("seq") % 2
    for k, (ref, g) in enumerate(((own_ref, core), (other_ref, 1 - core))):
        tiles[k] = ref[...].astype(F32)
        for m in range(modes):
            flat[tile(g * modes + m), :] = tiles[k, pl.ds(m * 3 * GROUP + 2, GROUP, stride=3), :]
    for b in range(blocks):
        row = b // GROUP * modes * GROUP + b % GROUP
        found = flat[pl.ds(row, modes, stride=GROUP), :]
        out_ref[:, pl.ds(b * LANES, LANES)] = found
        wire_ref[:, pl.ds(b * LANES, LANES)] = found.astype(BF16)


def final_kernel(
    modes, blocks, tokens, own_ref, other_ref, near_ref, fwd_ref, bwd_hbm, dec_ref, gain_ref, upstream_hbm,
    grad_gated_hbm, grad_value_hbm, tiles, zts, gts, bwd_ref, upstream_ref, grad_gated_ref,
    grad_value_ref, in_sems, sems
):
    groups = blocks // GROUP
    half = GROUP * LANES
    own_copies = []
    for g in range(groups):
        rows = pl.ds(g * tokens * GROUP, tokens * GROUP)
        own_copies.append(
            pltpu.make_async_copy(bwd_hbm.at[rows, :], bwd_ref.at[rows, :], in_sems.at[g])
        )
    upstream_copy = pltpu.make_async_copy(upstream_hbm, upstream_ref, in_sems.at[groups])
    for copy in [own_copies[0], upstream_copy] + own_copies[1:]:
        copy.start()
    tiles[0] = own_ref[...].astype(F32)
    tiles[1] = other_ref[...].astype(F32)
    odd = jnp.broadcast_to(lax.axis_index("seq") % 2, (GROUP, LANES)) == 1
    copies = []

    def send(src, dst, first, size):
        rows = pl.ds(first * LANES, size * LANES)
        copy = pltpu.make_async_copy(src.at[rows, :], dst.at[rows, :], sems.at[len(copies)])
        copy.start()
        copies.append(copy)

    for g in range(groups):
        decay = [dec_ref[tile(g * modes + m), :] for m in range(modes)]
        left, right = [], []
        for m in range(modes):
            rows = pl.ds(m * 3 * GROUP + g, GROUP, stride=3)
            scale = gain_ref[tile(g * modes + m), :] * decay[m]
            jump = decay[m]
            for _ in range(tokens.bit_length() - 1):
                jump = jump * jump
            direct = tiles[0, rows, :] * scale
            across = (tiles[1, rows, :] * jump + near_ref[tile(g * modes + m), :]) * scale
            left.append(jnp.where(odd, across, direct))
            right.append(jnp.where(odd, direct, across))

        def ahead(i, x, g=g, decay=decay):
            for u in range(FINAL_UNROLL):
                t = i * FINAL_UNROLL + u
                zts[g][tile(t), :] = fwd_ref[tile(g * tokens + t), :] + total(list(x))
                x = [a * v for a, v in zip(decay, x)]
            return x

        def behind(i, y, g=g, decay=decay):
            for u in range(FINAL_UNROLL):
                s = tokens - 1 - i * FINAL_UNROLL - u
                gts[g][tile(s), :] = bwd_ref[tile(g * tokens + s), :] + total(list(y))
                y = [a * v for a, v in zip(decay, y)]
            return y

        lax.fori_loop(0, tokens // FINAL_UNROLL, ahead, left)
        if g == 0:
            upstream_copy.wait()
        for j in range(GROUP):
            rows = pl.ds(g * half + j * LANES, LANES)
            z = transposed(zts[g][pl.ds(j, tokens, stride=GROUP), :].astype(BF16))
            grad_value_ref[rows, :] = (upstream_ref[rows, :].astype(F32) * z).astype(BF16)
        send(grad_value_ref, grad_value_hbm, g * GROUP, GROUP)
        own_copies[g].wait()
        lax.fori_loop(0, tokens // FINAL_UNROLL, behind, right)
        for j in range(GROUP):
            rows = pl.ds(g * half + j * LANES, LANES)
            back = transposed(gts[g][pl.ds(j, tokens, stride=GROUP), :].astype(BF16))
            grad_gated_ref[rows, :] = back.astype(BF16)
            if j % 4 == 3:
                send(grad_gated_ref, grad_gated_hbm, g * GROUP + j - 3, 4)
    for copy in copies:
        copy.wait()


def local(gated, value, upstream, residue, rate, skip_weight):
    channels, tokens = gated.shape
    modes = rate.shape[1]
    chunks = lax.axis_size("seq")
    blocks = channels // LANES
    pairs = modes * blocks
    groups = blocks // GROUP
    assert tokens == LANES == UNROLL * GROUP and pairs == 2 * chunks
    assert blocks == 2 * GROUP and modes == 2 * PART and chunks % (2 * SCAN_UNROLL) == 0
    rate_t, residue_t, skip = rate.T, residue.T, skip_weight[None, :]
    vmem = pl.BlockSpec(memory_space=pltpu.VMEM)
    hbm = pl.BlockSpec(memory_space=pltpu.HBM)
    cells = modes * channels * tokens

    def call(kernel, specs, out_specs, shapes, scratch, flops, size, limit=16 * 2**20):
        return pl.pallas_call(
            kernel,
            in_specs=specs,
            out_specs=out_specs,
            out_shape=[jax.ShapeDtypeStruct(*shape) for shape in shapes],
            scratch_shapes=scratch,
            compiler_params=pltpu.CompilerParams(vmem_limit_bytes=limit),
            cost_estimate=pl.CostEstimate(flops=flops, bytes_accessed=size, transcendentals=0),
        )

    native = ((channels, tokens), BF16)
    signal = ((tokens * blocks, LANES), F32)
    per_mode = ((pairs, LANES), F32)
    wire = (chunks * 2 * KINDS, LANES)
    answer = (chunks * 3, LANES)
    one = pltpu.VMEM((tokens * GROUP, LANES), F32)
    raw = pltpu.VMEM(*native)
    unpacked = pltpu.VMEM(wire, F32)
    staged = pltpu.VMEM(wire, BF16)
    flat = pltpu.VMEM(*per_mode)
    sems = lambda count: pltpu.SemaphoreType.DMA((count,))
    states, dz, edge = call(
        functools.partial(state_kernel, modes, blocks, tokens),
        [hbm] * 4,
        [hbm] * 3,
        [(wire, BF16), native, per_mode],
        [raw, raw, raw, raw, pltpu.VMEM((modes, channels), F32), [one] * groups, [one] * groups]
        + [flat, unpacked, staged, flat, sems(3 * groups + 1), sems(modes // STATE_PART)]
        + [sems(groups + 1)],
        5 * cells,
        8 * channels * tokens,
        LIMIT,
    )(gated, value, upstream, rate_t)

    def exchange(array):
        rows = array.shape[0] // chunks
        parts = array.reshape(chunks // 2, 3, 2 * rows // 3, LANES)
        members = [list(range(core, chunks, 2)) for core in range(2)]
        return lax.all_to_all(
            parts, "seq", split_axis=0, concat_axis=0, axis_index_groups=members, tiled=True
        ).reshape(array.shape)

    def beside(array):
        return lax.ppermute(array, "seq", [(d, d ^ 1) for d in range(chunks)])

    states, gated_held = lax.optimization_barrier((states, gated))
    fwd, decay, gain, lam = call(
        functools.partial(ahead_kernel, modes, blocks, tokens),
        [vmem] * 4,
        [vmem] * 4,
        [signal, per_mode, per_mode, ((4, LANES), F32)],
        [one],
        4 * cells,
        6 * channels * tokens,
    )(gated_held, rate_t, residue_t, skip)
    fwd, edge, dz = lax.optimization_barrier((fwd, edge, dz))
    (bwd,) = call(
        functools.partial(behind_kernel, modes, blocks, tokens),
        [vmem] * 4,
        [vmem],
        [signal],
        [one],
        4 * cells,
        6 * channels * tokens,
    )(dz, decay, gain, skip)
    heard, fwd, bwd, lam, near = lax.optimization_barrier(
        (exchange(states), fwd, bwd, lam, beside(edge))
    )
    heard_other = beside(heard)
    chained = pltpu.VMEM((2,) + wire, F32)
    (entering,) = call(
        functools.partial(scan_kernel, chunks, tokens),
        [vmem] * 3,
        [vmem],
        [(answer, BF16)],
        [chained, pltpu.VMEM((2,) + answer, F32), pltpu.VMEM((4, LANES), F32)],
        16 * chunks * GROUP * LANES,
        8 * chunks * GROUP * LANES,
    )(heard, heard_other, lam)
    returned = exchange(entering)
    returned_other = beside(returned)
    grad_own, grad_wire = call(
        functools.partial(residue_kernel, modes, blocks),
        [vmem] * 2,
        [vmem] * 2,
        [((modes, channels), F32), ((modes, channels), BF16)],
        [pltpu.VMEM((2,) + answer, F32), flat],
        modes * channels,
        8 * modes * channels,
    )(returned, returned_other)
    grad_other = lax.ppermute(grad_wire, "ch", [(0, 1), (1, 0)]).astype(F32)
    grad_gated, grad_value = call(
        functools.partial(final_kernel, modes, blocks, tokens),
        [vmem, vmem, vmem, vmem, hbm, vmem, vmem, hbm],
        [hbm] * 2,
        [native, native],
        [pltpu.VMEM((2,) + answer, F32), [one] * groups, [one] * groups]
        + [pltpu.VMEM(*signal), raw, raw, raw]
        + [sems(groups + 1), sems(3 * groups)],
        4 * cells,
        14 * channels * tokens,
    )(returned, returned_other, near, fwd, bwd, decay, gain, upstream)
    low = lax.axis_index("ch") == 0
    grad_res = jnp.concatenate(
        [jnp.where(low, grad_own, grad_other), jnp.where(low, grad_other, grad_own)], axis=1
    )
    return (grad_gated, grad_value, grad_res.T)


def solution(mesh):
    return jax.shard_map(
        local,
        mesh=mesh,
        in_specs=(P("ch", "seq"), P("ch", "seq"), P("ch", "seq"), P(), P(), P()),
        out_specs=(P("ch", "seq"), P("ch", "seq"), P()),
        check_vma=False,
    )
```

```python
import functools

import jax
import jax.numpy as jnp
from jax import lax
from jax.experimental import pallas as pl
from jax.experimental.pallas import tpu as pltpu
from jax.sharding import PartitionSpec as P

F32 = jnp.float32
BF16 = jnp.bfloat16
LANES = 128
GROUP = 8
KINDS = 3
PART, UNROLL = 8, 16
FINAL_UNROLL = 16
SCAN_UNROLL = 4
STATE_PART, STATE_UNROLL, RUN = 4, 32, 4
LIMIT = 56 * 2**20


def transposed(block):
    return block.astype(F32).T


def spread_modes(src_ref, dst_ref, first, modes, blocks):
    for b in range(blocks):
        start = pl.multiple_of(first + b * LANES, LANES)
        row = b // GROUP * modes * GROUP + b % GROUP
        dst_ref[pl.ds(row, modes, stride=GROUP), :] = src_ref[:, pl.ds(start, LANES)]


def tile(index):
    return pl.ds(pl.multiple_of(index * GROUP, GROUP), GROUP)


def put_signal(signal_ref, gt, b, j, tokens):
    gt[pl.ds(j, tokens, stride=GROUP), :] = transposed(signal_ref[pl.ds(b * LANES, LANES), :])


def put_dz(value_ref, upstream_ref, dz_ref, dzt, b, j, tokens):
    rows = pl.ds(b * LANES, LANES)
    dz = (upstream_ref[rows, :].astype(F32) * value_ref[rows, :].astype(F32)).astype(BF16)
    dz_ref[rows, :] = dz
    dzt[pl.ds(j, tokens, stride=GROUP), :] = transposed(dz)


def total(terms):
    while len(terms) > 1:
        pairs = [a + b for a, b in zip(terms[::2], terms[1::2])]
        terms = pairs + ([terms[-1]] if len(terms) % 2 else [])
    return terms[0]


def power(base, exponent):
    result = base
    for _ in range(exponent - 1):
        result = result * base
    return result


def horner(base, terms):
    result = terms[0]
    for term in terms[1:]:
        result = result * base + term
    return result


def state_kernel(
    modes, blocks, tokens, gated_hbm, value_hbm, upstream_hbm, rate_hbm, out_hbm, dz_hbm,
    gated_ref, value_ref, upstream_ref, dz_ref, rate_ref, gts, dzts, lam, pack, stage, sems, out_sems, dz_sems
):
    half = GROUP * LANES
    groups = blocks // GROUP
    start = pl.multiple_of(lax.axis_index("ch") * (blocks * LANES), LANES)
    rate_copy = pltpu.make_async_copy(
        rate_hbm.at[:, pl.ds(start, blocks * LANES)], rate_ref, sems.at[3 * groups]
    )
    copies = []
    for g in range(groups):
        rows = pl.ds(g * half, half)
        pairs = ((gated_hbm, gated_ref), (upstream_hbm, upstream_ref), (value_hbm, value_ref))
        copies.append(
            [
                pltpu.make_async_copy(src.at[rows, :], dst.at[rows, :], sems.at[3 * g + k])
                for k, (src, dst) in enumerate(pairs)
            ]
        )
    for copy in copies[0] + [rate_copy]:
        copy.start()
    copies[0][0].wait()
    for j in range(GROUP):
        put_signal(gated_ref, gts[0], j, j, tokens)
    copies[0][1].wait()
    copies[0][2].wait()
    for j in range(GROUP):
        put_dz(value_ref, upstream_ref, dz_ref, dzts[0], j, j, tokens)
    for part in copies[1:]:
        for copy in part:
            copy.start()
    rate_copy.wait()
    spread_modes(rate_ref, lam, 0, modes, blocks)
    zero = jnp.zeros((GROUP, LANES), F32)
    sent, late = [], []
    for g in range(groups):
        gt, dzt = gts[g], dzts[g]
        if g:
            for copy in copies[g]:
                copy.wait()
            for j in range(GROUP):
                put_signal(gated_ref, gt, g * GROUP + j, j, tokens)
                put_dz(value_ref, upstream_ref, dz_ref, dzt, g * GROUP + j, j, tokens)
        rows = pl.ds(g * half, half)
        copy = pltpu.make_async_copy(dz_ref.at[rows, :], dz_hbm.at[rows, :], dz_sems.at[g])
        copy.start()
        late.append(copy)
        lags = None
        for m0 in range(0, modes, STATE_PART):
            some = range(m0, m0 + STATE_PART)
            decay = [jnp.exp(-lam[tile(g * modes + m), :]) for m in some]
            jump = [power(a, RUN) for a in decay]

            def body(i, carry, gt=gt, dzt=dzt, decay=decay, jump=jump, first=m0 == 0):
                x, y, own, reach, lags = carry
                for u in range(STATE_UNROLL // RUN):
                    t = i * STATE_UNROLL + u * RUN
                    gs = [gt[tile(t + k), :] for k in range(RUN)]
                    ds = [dzt[tile(t + k), :] for k in range(RUN)]
                    if first:
                        lags = [
                            c + total([d * v for d, v in zip(ds[k:], gs)])
                            for k, c in enumerate(lags)
                        ]
                    ends = [horner(a, gs) for a in decay]
                    starts = [horner(a, ds[::-1]) for a in decay]
                    own = [o + v * w for o, v, w in zip(own, x, starts)]
                    y = [v + p * w for v, p, w in zip(y, reach, starts)]
                    x = [a * v + w for a, v, w in zip(jump, x, ends)]
                    reach = [a * p for a, p in zip(jump, reach)]
                return x, y, own, reach, lags

            zeros = [zero] * STATE_PART
            ones = [zero + 1.0] * STATE_PART
            carry = (zeros, zeros, zeros, ones, [zero] * RUN if m0 == 0 else [])
            x, y, own, _, found = lax.fori_loop(0, tokens // STATE_UNROLL, body, carry)
            lags = found if m0 == 0 else lags
            for k in range(STATE_PART):
                base = (m0 + k) * GROUP * 2 * KINDS + g * KINDS
                term = decay[k] * own[k] + horner(decay[k], lags[::-1])
                for kind, rows in enumerate((x[k], y[k], term)):
                    pack[pl.ds(base + kind, GROUP, stride=2 * KINDS), :] = rows
            if g < groups - 1:
                continue
            rows = pl.ds(m0 * GROUP * 2 * KINDS, STATE_PART * GROUP * 2 * KINDS)
            stage[rows, :] = pack[rows, :].astype(BF16)
            copy = pltpu.make_async_copy(
                stage.at[rows, :], out_hbm.at[rows, :], out_sems.at[len(sent)]
            )
            copy.start()
            sent.append(copy)
    for copy in sent + late:
        copy.wait()


def own_sums(modes, tokens, g, signal, out_ref, dec_ref, gain_ref, skip, order):
    zero = jnp.zeros((GROUP, LANES), F32)
    for m0 in range(0, modes, PART):
        decay = [dec_ref[tile(g * modes + m), :] for m in range(m0, m0 + PART)]
        gain = [gain_ref[tile(g * modes + m), :] for m in range(m0, m0 + PART)]

        def body(i, x, m0=m0, decay=decay, gain=gain):
            for u in range(UNROLL):
                t = order(i * UNROLL + u)
                at = tile(g * tokens + t)
                v = signal[tile(t), :]
                x = [a * w + v for a, w in zip(decay, x)]
                known = out_ref[at, :] if m0 else skip * v
                out_ref[at, :] = total([r * w for r, w in zip(gain, x)] + [known])
            return x

        lax.fori_loop(0, tokens // UNROLL, body, [zero] * PART)


def skip_of(skip_ref, first, g):
    parts = [
        skip_ref[:, pl.ds(pl.multiple_of(first + (g * GROUP + j) * LANES, LANES), LANES)]
        for j in range(GROUP)
    ]
    return jnp.concatenate(parts, axis=0)


def ahead_kernel(
    modes, blocks, tokens, gated_ref, rate_ref, res_ref, skip_ref,
    fwd_ref, dec_ref, gain_ref, lam_ref, gt
):
    first = lax.axis_index("ch") * (blocks * LANES)
    spread_modes(rate_ref, dec_ref, first, modes, blocks)
    spread_modes(res_ref, gain_ref, first, modes, blocks)
    for h in range(2):
        for g in range(blocks // GROUP):
            row = g * modes * GROUP + lax.axis_index("seq") // 2 * 2 + h
            own = dec_ref[pl.ds(row, 1), :]
            lam_ref[pl.ds(2 * h + g, 1), :] = own
    dec_ref[...] = jnp.exp(-dec_ref[...])
    for g in range(blocks // GROUP):
        for j in range(GROUP):
            put_signal(gated_ref, gt, g * GROUP + j, j, tokens)
        skip = skip_of(skip_ref, first, g)
        own_sums(modes, tokens, g, gt, fwd_ref, dec_ref, gain_ref, skip, lambda t: t)


def behind_kernel(modes, blocks, tokens, dz_ref, dec_ref, gain_ref, skip_ref, bwd_ref, dzt):
    first = lax.axis_index("ch") * (blocks * LANES)
    for g in range(blocks // GROUP):
        for j in range(GROUP):
            put_signal(dz_ref, dzt, g * GROUP + j, j, tokens)
        skip = skip_of(skip_ref, first, g)
        order = lambda t: tokens - 1 - t
        own_sums(modes, tokens, g, dzt, bwd_ref, dec_ref, gain_ref, skip, order)


def scan_kernel(chunks, tokens, own_ref, other_ref, lam_ref, out_ref, sums, outs):
    core = lax.axis_index("seq") % 2
    chips = chunks // 2
    sums[core] = own_ref[...].astype(F32)
    sums[1 - core] = other_ref[...].astype(F32)
    lam = lam_ref[...]
    step = jnp.exp(lam * (-1.0 * tokens))
    zero = jnp.zeros((4, LANES), F32)

    def at(q, kind):
        return pl.ds(q * 4 * KINDS + kind, 4, stride=KINDS)

    def body(i, carry):
        x, y, own, cross = carry
        for u in range(SCAN_UNROLL):
            q, r = i * SCAN_UNROLL + u, chips - 1 - i * SCAN_UNROLL - u
            for place in range(2):
                outs[place, at(q, 0), :] = x
                outs[1 - place, at(r, 1), :] = y
                own = own + sums[place, at(q, 2), :]
                cross = cross + sums[place, at(q, 1), :] * x
                x = step * x + sums[place, at(q, 0), :]
                y = step * y + sums[1 - place, at(r, 1), :]
        return x, y, own, cross

    _, _, own, cross = lax.fori_loop(0, chips // SCAN_UNROLL, body, (zero, zero, zero, zero))
    grad = (own + cross * jnp.exp(-lam)) * (1.0 / (chunks * tokens))
    for q in range(chips):
        outs[core, at(q, 2), :] = grad
    out_ref[...] = outs[core].astype(BF16)


def residue_kernel(modes, blocks, in_ref, out_ref, wire_ref, tiles, flat):
    tiles[...] = in_ref[...].astype(F32)
    for r in range(modes * blocks // GROUP):
        base = r % modes * GROUP * 2 * KINDS + r // modes * KINDS
        flat[pl.ds(r * GROUP, GROUP), :] = tiles[pl.ds(base + 2, GROUP, stride=2 * KINDS), :]
    for b in range(blocks):
        row = b // GROUP * modes * GROUP + b % GROUP
        found = flat[pl.ds(row, modes, stride=GROUP), :]
        out_ref[:, pl.ds(b * LANES, LANES)] = found
        wire_ref[:, pl.ds(b * LANES, LANES)] = found.astype(BF16)


def final_kernel(
    modes, blocks, tokens, in_ref, fwd_ref, bwd_hbm, dec_ref, gain_ref, upstream_hbm, residue_ref,
    grad_gated_hbm, grad_value_hbm, grad_residue_hbm, tiles, zts, gts, bwd_ref, upstream_ref, grad_gated_ref,
    grad_value_ref, in_sems, sems
):
    groups = blocks // GROUP
    half = GROUP * LANES
    own_copies = []
    for g in range(groups):
        rows = pl.ds(g * tokens * GROUP, tokens * GROUP)
        own_copies.append(
            pltpu.make_async_copy(bwd_hbm.at[rows, :], bwd_ref.at[rows, :], in_sems.at[g])
        )
    upstream_copy = pltpu.make_async_copy(upstream_hbm, upstream_ref, in_sems.at[groups])
    channels = blocks * LANES
    start = pl.multiple_of(lax.axis_index("ch") * channels, LANES)
    residue_copy = pltpu.make_async_copy(
        residue_ref, grad_residue_hbm.at[:, pl.ds(start, channels)], in_sems.at[groups + 1]
    )
    for copy in [own_copies[0], upstream_copy] + own_copies[1:] + [residue_copy]:
        copy.start()
    tiles[...] = in_ref[...].astype(F32)
    copies = []

    def send(src, dst, first, size):
        rows = pl.ds(first * LANES, size * LANES)
        copy = pltpu.make_async_copy(src.at[rows, :], dst.at[rows, :], sems.at[len(copies)])
        copy.start()
        copies.append(copy)

    for g in range(groups):
        decay = [dec_ref[tile(g * modes + m), :] for m in range(modes)]
        scale = [gain_ref[tile(g * modes + m), :] * decay[m] for m in range(modes)]

        def entering(kind, g=g, scale=scale):
            bases = [m * GROUP * 2 * KINDS + g * KINDS + kind for m in range(modes)]
            return [
                tiles[pl.ds(base, GROUP, stride=2 * KINDS), :] * a for base, a in zip(bases, scale)
            ]

        def ahead(i, x, g=g, decay=decay):
            for u in range(FINAL_UNROLL):
                t = i * FINAL_UNROLL + u
                zts[g][tile(t), :] = fwd_ref[tile(g * tokens + t), :] + total(list(x))
                x = [a * v for a, v in zip(decay, x)]
            return x

        def behind(i, y, g=g, decay=decay):
            for u in range(FINAL_UNROLL):
                s = tokens - 1 - i * FINAL_UNROLL - u
                gts[g][tile(s), :] = bwd_ref[tile(g * tokens + s), :] + total(list(y))
                y = [a * v for a, v in zip(decay, y)]
            return y

        lax.fori_loop(0, tokens // FINAL_UNROLL, ahead, entering(0))
        if g == 0:
            upstream_copy.wait()
        for j in range(GROUP):
            rows = pl.ds(g * half + j * LANES, LANES)
            z = transposed(zts[g][pl.ds(j, tokens, stride=GROUP), :].astype(BF16))
            grad_value_ref[rows, :] = (upstream_ref[rows, :].astype(F32) * z).astype(BF16)
        send(grad_value_ref, grad_value_hbm, g * GROUP, GROUP)
        own_copies[g].wait()
        lax.fori_loop(0, tokens // FINAL_UNROLL, behind, entering(1))
        for j in range(GROUP):
            rows = pl.ds(g * half + j * LANES, LANES)
            back = transposed(gts[g][pl.ds(j, tokens, stride=GROUP), :].astype(BF16))
            grad_gated_ref[rows, :] = back.astype(BF16)
            if j % 4 == 3:
                send(grad_gated_ref, grad_gated_hbm, g * GROUP + j - 3, 4)
    for copy in copies + [residue_copy]:
        copy.wait()


def local(gated, value, upstream, residue, rate, skip_weight):
    channels, tokens = gated.shape
    modes = rate.shape[1]
    chunks = lax.axis_size("seq")
    blocks = channels // LANES
    pairs = modes * blocks
    groups = blocks // GROUP
    assert tokens == LANES == UNROLL * GROUP and pairs == 2 * chunks
    assert blocks == 2 * GROUP and modes == 2 * PART and chunks % (2 * SCAN_UNROLL) == 0
    rate_t, residue_t, skip = rate.T, residue.T, skip_weight[None, :]
    vmem = pl.BlockSpec(memory_space=pltpu.VMEM)
    hbm = pl.BlockSpec(memory_space=pltpu.HBM)
    cells = modes * channels * tokens

    def call(kernel, specs, out_specs, shapes, scratch, flops, size, limit=16 * 2**20):
        return pl.pallas_call(
            kernel,
            in_specs=specs,
            out_specs=out_specs,
            out_shape=[jax.ShapeDtypeStruct(*shape) for shape in shapes],
            scratch_shapes=scratch,
            compiler_params=pltpu.CompilerParams(vmem_limit_bytes=limit),
            cost_estimate=pl.CostEstimate(flops=flops, bytes_accessed=size, transcendentals=0),
        )

    native = ((channels, tokens), BF16)
    signal = ((tokens * blocks, LANES), F32)
    per_mode = ((pairs, LANES), F32)
    wire = (chunks * 2 * KINDS, LANES)
    one = pltpu.VMEM((tokens * GROUP, LANES), F32)
    raw = pltpu.VMEM(*native)
    unpacked = pltpu.VMEM(wire, F32)
    staged = pltpu.VMEM(wire, BF16)
    flat = pltpu.VMEM(*per_mode)
    sems = lambda count: pltpu.SemaphoreType.DMA((count,))
    states, dz = call(
        functools.partial(state_kernel, modes, blocks, tokens),
        [hbm] * 4,
        [hbm] * 2,
        [(wire, BF16), native],
        [raw, raw, raw, raw, pltpu.VMEM((modes, channels), F32), [one] * groups, [one] * groups]
        + [flat, unpacked, staged, sems(3 * groups + 1), sems(modes // STATE_PART)]
        + [sems(groups)],
        5 * cells,
        8 * channels * tokens,
        LIMIT,
    )(gated, value, upstream, rate_t)

    def exchange(array):
        array = array.reshape(chunks // 2, KINDS, 4, LANES)
        members = [list(range(core, chunks, 2)) for core in range(2)]
        return lax.all_to_all(
            array, "seq", split_axis=0, concat_axis=0, axis_index_groups=members, tiled=True
        ).reshape(wire)

    states, gated_held = lax.optimization_barrier((states, gated))
    fwd, decay, gain, lam = call(
        functools.partial(ahead_kernel, modes, blocks, tokens),
        [vmem] * 4,
        [vmem] * 4,
        [signal, per_mode, per_mode, ((4, LANES), F32)],
        [one],
        4 * cells,
        6 * channels * tokens,
    )(gated_held, rate_t, residue_t, skip)
    fwd, dz = lax.optimization_barrier((fwd, dz))
    (bwd,) = call(
        functools.partial(behind_kernel, modes, blocks, tokens),
        [vmem] * 4,
        [vmem],
        [signal],
        [one],
        4 * cells,
        6 * channels * tokens,
    )(dz, decay, gain, skip)
    heard, fwd, bwd, lam = lax.optimization_barrier((exchange(states), fwd, bwd, lam))
    heard_other = lax.ppermute(heard, "seq", [(d, d ^ 1) for d in range(chunks)])
    chained = pltpu.VMEM((2,) + wire, F32)
    (entering,) = call(
        functools.partial(scan_kernel, chunks, tokens),
        [vmem] * 3,
        [vmem],
        [(wire, BF16)],
        [chained, chained],
        16 * chunks * GROUP * LANES,
        8 * chunks * GROUP * LANES,
    )(heard, heard_other, lam)
    returned = exchange(entering)
    grad_own, grad_wire = call(
        functools.partial(residue_kernel, modes, blocks),
        [vmem],
        [vmem] * 2,
        [((modes, channels), F32), ((modes, channels), BF16)],
        [unpacked, flat],
        modes * channels,
        8 * modes * channels,
    )(returned)
    grad_other = lax.ppermute(grad_wire, "ch", [(0, 1), (1, 0)]).astype(F32)
    grad_gated, grad_value, grad_res = call(
        functools.partial(final_kernel, modes, blocks, tokens),
        [vmem, vmem, hbm, vmem, vmem, hbm, vmem],
        [hbm] * 3,
        [native, native, ((modes, residue.shape[0]), F32)],
        [unpacked, [one] * groups, [one] * groups, pltpu.VMEM(*signal), raw, raw, raw]
        + [sems(groups + 2), sems(3 * groups)],
        4 * cells,
        14 * channels * tokens,
    )(returned, fwd, bwd, decay, gain, upstream, grad_own)
    place = (1 - lax.axis_index("ch")) * channels
    grad_res = lax.dynamic_update_slice(grad_res, grad_other, (0, place))
    return (grad_gated, grad_value, grad_res.T)


def solution(mesh):
    return jax.shard_map(
        local,
        mesh=mesh,
        in_specs=(P("ch", "seq"), P("ch", "seq"), P("ch", "seq"), P(), P(), P()),
        out_specs=(P("ch", "seq"), P("ch", "seq"), P()),
        check_vma=False,
    )
```

```python
import functools

import jax
import jax.numpy as jnp
from jax import lax
from jax.experimental import pallas as pl
from jax.experimental.pallas import tpu as pltpu
from jax.sharding import PartitionSpec as P

F32 = jnp.float32
BF16 = jnp.bfloat16
LANES = 128
GROUP = 8
KINDS = 3
PART, UNROLL = 8, 16
FINAL_UNROLL = 16
RUN_OF_CHIPS = 8
STATE_PART, STATE_UNROLL, RUN = 4, 32, 4
LIMIT = 56 * 2**20


def transposed(block):
    return block.astype(F32).T


def spread_modes(src_ref, dst_ref, first, modes, blocks):
    for b in range(blocks):
        start = pl.multiple_of(first + b * LANES, LANES)
        row = b // GROUP * modes * GROUP + b % GROUP
        dst_ref[pl.ds(row, modes, stride=GROUP), :] = src_ref[:, pl.ds(start, LANES)]


def tile(index):
    return pl.ds(pl.multiple_of(index * GROUP, GROUP), GROUP)


def put_signal(signal_ref, gt, b, j, tokens):
    gt[pl.ds(j, tokens, stride=GROUP), :] = transposed(signal_ref[pl.ds(b * LANES, LANES), :])


def put_dz(value_ref, upstream_ref, dz_ref, dzt, b, j, tokens):
    rows = pl.ds(b * LANES, LANES)
    dz = (upstream_ref[rows, :].astype(F32) * value_ref[rows, :].astype(F32)).astype(BF16)
    dz_ref[rows, :] = dz
    dzt[pl.ds(j, tokens, stride=GROUP), :] = transposed(dz)


def total(terms):
    while len(terms) > 1:
        pairs = [a + b for a, b in zip(terms[::2], terms[1::2])]
        terms = pairs + ([terms[-1]] if len(terms) % 2 else [])
    return terms[0]


def power(base, exponent):
    result = base
    for _ in range(exponent - 1):
        result = result * base
    return result


def horner(base, terms):
    result = terms[0]
    for term in terms[1:]:
        result = result * base + term
    return result


def state_kernel(
    modes, blocks, tokens, gated_hbm, value_hbm, upstream_hbm, rate_hbm, out_hbm, dz_hbm,
    gated_ref, value_ref, upstream_ref, dz_ref, rate_ref, gts, dzts, lam, pack, stage, sems, out_sems, dz_sems
):
    half = GROUP * LANES
    groups = blocks // GROUP
    start = pl.multiple_of(lax.axis_index("ch") * (blocks * LANES), LANES)
    rate_copy = pltpu.make_async_copy(
        rate_hbm.at[:, pl.ds(start, blocks * LANES)], rate_ref, sems.at[3 * groups]
    )
    copies = []
    for g in range(groups):
        rows = pl.ds(g * half, half)
        pairs = ((gated_hbm, gated_ref), (upstream_hbm, upstream_ref), (value_hbm, value_ref))
        copies.append(
            [
                pltpu.make_async_copy(src.at[rows, :], dst.at[rows, :], sems.at[3 * g + k])
                for k, (src, dst) in enumerate(pairs)
            ]
        )
    for copy in copies[0] + [rate_copy]:
        copy.start()
    copies[0][0].wait()
    for j in range(GROUP):
        put_signal(gated_ref, gts[0], j, j, tokens)
    copies[0][1].wait()
    copies[0][2].wait()
    for j in range(GROUP):
        put_dz(value_ref, upstream_ref, dz_ref, dzts[0], j, j, tokens)
    for part in copies[1:]:
        for copy in part:
            copy.start()
    rate_copy.wait()
    spread_modes(rate_ref, lam, 0, modes, blocks)
    zero = jnp.zeros((GROUP, LANES), F32)
    sent, late = [], []
    for g in range(groups):
        gt, dzt = gts[g], dzts[g]
        if g:
            for copy in copies[g]:
                copy.wait()
            for j in range(GROUP):
                put_signal(gated_ref, gt, g * GROUP + j, j, tokens)
                put_dz(value_ref, upstream_ref, dz_ref, dzt, g * GROUP + j, j, tokens)
        rows = pl.ds(g * half, half)
        copy = pltpu.make_async_copy(dz_ref.at[rows, :], dz_hbm.at[rows, :], dz_sems.at[g])
        copy.start()
        late.append(copy)
        lags = None
        for m0 in range(0, modes, STATE_PART):
            some = range(m0, m0 + STATE_PART)
            decay = [jnp.exp(-lam[tile(g * modes + m), :]) for m in some]
            jump = [power(a, RUN) for a in decay]

            def body(i, carry, gt=gt, dzt=dzt, decay=decay, jump=jump, first=m0 == 0):
                x, y, own, reach, lags = carry
                for u in range(STATE_UNROLL // RUN):
                    t = i * STATE_UNROLL + u * RUN
                    gs = [gt[tile(t + k), :] for k in range(RUN)]
                    ds = [dzt[tile(t + k), :] for k in range(RUN)]
                    if first:
                        lags = [
                            c + total([d * v for d, v in zip(ds[k:], gs)])
                            for k, c in enumerate(lags)
                        ]
                    ends = [horner(a, gs) for a in decay]
                    starts = [horner(a, ds[::-1]) for a in decay]
                    own = [o + v * w for o, v, w in zip(own, x, starts)]
                    y = [v + p * w for v, p, w in zip(y, reach, starts)]
                    x = [a * v + w for a, v, w in zip(jump, x, ends)]
                    reach = [a * p for a, p in zip(jump, reach)]
                return x, y, own, reach, lags

            zeros = [zero] * STATE_PART
            ones = [zero + 1.0] * STATE_PART
            carry = (zeros, zeros, zeros, ones, [zero] * RUN if m0 == 0 else [])
            x, y, own, _, found = lax.fori_loop(0, tokens // STATE_UNROLL, body, carry)
            lags = found if m0 == 0 else lags
            for k in range(STATE_PART):
                base = (m0 + k) * GROUP * 2 * KINDS + g * KINDS
                term = decay[k] * own[k] + horner(decay[k], lags[::-1])
                for kind, rows in enumerate((x[k], y[k], term)):
                    pack[pl.ds(base + kind, GROUP, stride=2 * KINDS), :] = rows
            if g < groups - 1:
                continue
            rows = pl.ds(m0 * GROUP * 2 * KINDS, STATE_PART * GROUP * 2 * KINDS)
            stage[rows, :] = pack[rows, :].astype(BF16)
            copy = pltpu.make_async_copy(
                stage.at[rows, :], out_hbm.at[rows, :], out_sems.at[len(sent)]
            )
            copy.start()
            sent.append(copy)
    for copy in sent + late:
        copy.wait()


def own_sums(modes, tokens, g, signal, out_ref, dec_ref, gain_ref, skip, order):
    zero = jnp.zeros((GROUP, LANES), F32)
    for m0 in range(0, modes, PART):
        decay = [dec_ref[tile(g * modes + m), :] for m in range(m0, m0 + PART)]
        gain = [gain_ref[tile(g * modes + m), :] for m in range(m0, m0 + PART)]

        def body(i, x, m0=m0, decay=decay, gain=gain):
            for u in range(UNROLL):
                t = order(i * UNROLL + u)
                at = tile(g * tokens + t)
                v = signal[tile(t), :]
                x = [a * w + v for a, w in zip(decay, x)]
                known = out_ref[at, :] if m0 else skip * v
                out_ref[at, :] = total([r * w for r, w in zip(gain, x)] + [known])
            return x

        lax.fori_loop(0, tokens // UNROLL, body, [zero] * PART)


def skip_of(skip_ref, first, g):
    parts = [
        skip_ref[:, pl.ds(pl.multiple_of(first + (g * GROUP + j) * LANES, LANES), LANES)]
        for j in range(GROUP)
    ]
    return jnp.concatenate(parts, axis=0)


def ahead_kernel(
    modes, blocks, tokens, gated_ref, rate_ref, res_ref, skip_ref,
    fwd_ref, dec_ref, gain_ref, lam_ref, gt
):
    first = lax.axis_index("ch") * (blocks * LANES)
    spread_modes(rate_ref, dec_ref, first, modes, blocks)
    spread_modes(res_ref, gain_ref, first, modes, blocks)
    for h in range(2):
        for g in range(blocks // GROUP):
            chip = lax.axis_index("seq") // 2
            row = g * modes * GROUP + (chip % RUN_OF_CHIPS * RUN_OF_CHIPS + chip // RUN_OF_CHIPS) * 2 + h
            own = dec_ref[pl.ds(row, 1), :]
            lam_ref[pl.ds(2 * h + g, 1), :] = own
    dec_ref[...] = jnp.exp(-dec_ref[...])
    for g in range(blocks // GROUP):
        for j in range(GROUP):
            put_signal(gated_ref, gt, g * GROUP + j, j, tokens)
        skip = skip_of(skip_ref, first, g)
        own_sums(modes, tokens, g, gt, fwd_ref, dec_ref, gain_ref, skip, lambda t: t)


def behind_kernel(modes, blocks, tokens, dz_ref, dec_ref, gain_ref, skip_ref, bwd_ref, dzt):
    first = lax.axis_index("ch") * (blocks * LANES)
    for g in range(blocks // GROUP):
        for j in range(GROUP):
            put_signal(dz_ref, dzt, g * GROUP + j, j, tokens)
        skip = skip_of(skip_ref, first, g)
        order = lambda t: tokens - 1 - t
        own_sums(modes, tokens, g, dzt, bwd_ref, dec_ref, gain_ref, skip, order)


def scan_kernel(chunks, tokens, own_ref, other_ref, lam_ref, out_ref, sums, outs):
    core = lax.axis_index("seq") % 2
    chips = chunks // 2
    sums[core] = own_ref[...].astype(F32)
    sums[1 - core] = other_ref[...].astype(F32)
    lam = lam_ref[...]
    step = jnp.exp(lam * (-1.0 * tokens))
    zero = jnp.zeros((4, LANES), F32)

    def at(q, kind):
        return pl.ds(q * 4 * KINDS + kind, 4, stride=KINDS)

    def body(i, carry):
        x, y, own, cross = carry
        for u in range(RUN_OF_CHIPS):
            q, r = u * RUN_OF_CHIPS + i, chips - 1 - u * RUN_OF_CHIPS - i
            for place in range(2):
                outs[place, at(q, 0), :] = x
                outs[1 - place, at(r, 1), :] = y
                own = own + sums[place, at(q, 2), :]
                cross = cross + sums[place, at(q, 1), :] * x
                x = step * x + sums[place, at(q, 0), :]
                y = step * y + sums[1 - place, at(r, 1), :]
        return x, y, own, cross

    _, _, own, cross = lax.fori_loop(0, RUN_OF_CHIPS, body, (zero, zero, zero, zero))
    grad = (own + cross * jnp.exp(-lam)) * (1.0 / (chunks * tokens))
    for q in range(chips):
        outs[core, at(q, 2), :] = grad
    out_ref[...] = outs[core].astype(BF16)


def residue_kernel(modes, blocks, in_ref, out_ref, wire_ref, tiles, flat):
    tiles[...] = in_ref[...].astype(F32)
    for r in range(modes * blocks // GROUP):
        base = r % modes * GROUP * 2 * KINDS + r // modes * KINDS
        flat[pl.ds(r * GROUP, GROUP), :] = tiles[pl.ds(base + 2, GROUP, stride=2 * KINDS), :]
    for b in range(blocks):
        row = b // GROUP * modes * GROUP + b % GROUP
        found = flat[pl.ds(row, modes, stride=GROUP), :]
        out_ref[:, pl.ds(b * LANES, LANES)] = found
        wire_ref[:, pl.ds(b * LANES, LANES)] = found.astype(BF16)


def final_kernel(
    modes, blocks, tokens, in_ref, fwd_ref, bwd_hbm, dec_ref, gain_ref, upstream_hbm, residue_ref,
    grad_gated_hbm, grad_value_hbm, grad_residue_hbm, tiles, zts, gts, bwd_ref, upstream_ref, grad_gated_ref,
    grad_value_ref, in_sems, sems
):
    groups = blocks // GROUP
    half = GROUP * LANES
    own_copies = []
    for g in range(groups):
        rows = pl.ds(g * tokens * GROUP, tokens * GROUP)
        own_copies.append(
            pltpu.make_async_copy(bwd_hbm.at[rows, :], bwd_ref.at[rows, :], in_sems.at[g])
        )
    upstream_copy = pltpu.make_async_copy(upstream_hbm, upstream_ref, in_sems.at[groups])
    channels = blocks * LANES
    start = pl.multiple_of(lax.axis_index("ch") * channels, LANES)
    residue_copy = pltpu.make_async_copy(
        residue_ref, grad_residue_hbm.at[:, pl.ds(start, channels)], in_sems.at[groups + 1]
    )
    for copy in [own_copies[0], upstream_copy] + own_copies[1:] + [residue_copy]:
        copy.start()
    tiles[...] = in_ref[...].astype(F32)
    copies = []

    def send(src, dst, first, size):
        rows = pl.ds(first * LANES, size * LANES)
        copy = pltpu.make_async_copy(src.at[rows, :], dst.at[rows, :], sems.at[len(copies)])
        copy.start()
        copies.append(copy)

    for g in range(groups):
        decay = [dec_ref[tile(g * modes + m), :] for m in range(modes)]
        scale = [gain_ref[tile(g * modes + m), :] * decay[m] for m in range(modes)]

        def entering(kind, g=g, scale=scale):
            bases = [m * GROUP * 2 * KINDS + g * KINDS + kind for m in range(modes)]
            return [
                tiles[pl.ds(base, GROUP, stride=2 * KINDS), :] * a for base, a in zip(bases, scale)
            ]

        def ahead(i, x, g=g, decay=decay):
            for u in range(FINAL_UNROLL):
                t = i * FINAL_UNROLL + u
                zts[g][tile(t), :] = fwd_ref[tile(g * tokens + t), :] + total(list(x))
                x = [a * v for a, v in zip(decay, x)]
            return x

        def behind(i, y, g=g, decay=decay):
            for u in range(FINAL_UNROLL):
                s = tokens - 1 - i * FINAL_UNROLL - u
                gts[g][tile(s), :] = bwd_ref[tile(g * tokens + s), :] + total(list(y))
                y = [a * v for a, v in zip(decay, y)]
            return y

        lax.fori_loop(0, tokens // FINAL_UNROLL, ahead, entering(0))
        if g == 0:
            upstream_copy.wait()
        for j in range(GROUP):
            rows = pl.ds(g * half + j * LANES, LANES)
            z = transposed(zts[g][pl.ds(j, tokens, stride=GROUP), :].astype(BF16))
            grad_value_ref[rows, :] = (upstream_ref[rows, :].astype(F32) * z).astype(BF16)
        send(grad_value_ref, grad_value_hbm, g * GROUP, GROUP)
        own_copies[g].wait()
        lax.fori_loop(0, tokens // FINAL_UNROLL, behind, entering(1))
        for j in range(GROUP):
            rows = pl.ds(g * half + j * LANES, LANES)
            back = transposed(gts[g][pl.ds(j, tokens, stride=GROUP), :].astype(BF16))
            grad_gated_ref[rows, :] = back.astype(BF16)
            if j % 4 == 3:
                send(grad_gated_ref, grad_gated_hbm, g * GROUP + j - 3, 4)
    for copy in copies + [residue_copy]:
        copy.wait()


def local(gated, value, upstream, residue, rate, skip_weight):
    channels, tokens = gated.shape
    modes = rate.shape[1]
    chunks = lax.axis_size("seq")
    blocks = channels // LANES
    pairs = modes * blocks
    groups = blocks // GROUP
    assert tokens == LANES == UNROLL * GROUP and pairs == 2 * chunks
    assert blocks == 2 * GROUP and modes == 2 * PART and chunks == 2 * RUN_OF_CHIPS**2
    rate_t, residue_t, skip = rate.T, residue.T, skip_weight[None, :]
    vmem = pl.BlockSpec(memory_space=pltpu.VMEM)
    hbm = pl.BlockSpec(memory_space=pltpu.HBM)
    cells = modes * channels * tokens

    def call(kernel, specs, out_specs, shapes, scratch, flops, size, limit=16 * 2**20):
        return pl.pallas_call(
            kernel,
            in_specs=specs,
            out_specs=out_specs,
            out_shape=[jax.ShapeDtypeStruct(*shape) for shape in shapes],
            scratch_shapes=scratch,
            compiler_params=pltpu.CompilerParams(vmem_limit_bytes=limit),
            cost_estimate=pl.CostEstimate(flops=flops, bytes_accessed=size, transcendentals=0),
        )

    native = ((channels, tokens), BF16)
    signal = ((tokens * blocks, LANES), F32)
    per_mode = ((pairs, LANES), F32)
    wire = (chunks * 2 * KINDS, LANES)
    one = pltpu.VMEM((tokens * GROUP, LANES), F32)
    raw = pltpu.VMEM(*native)
    unpacked = pltpu.VMEM(wire, F32)
    staged = pltpu.VMEM(wire, BF16)
    flat = pltpu.VMEM(*per_mode)
    sems = lambda count: pltpu.SemaphoreType.DMA((count,))
    states, dz = call(
        functools.partial(state_kernel, modes, blocks, tokens),
        [hbm] * 4,
        [hbm] * 2,
        [(wire, BF16), native],
        [raw, raw, raw, raw, pltpu.VMEM((modes, channels), F32), [one] * groups, [one] * groups]
        + [flat, unpacked, staged, sems(3 * groups + 1), sems(modes // STATE_PART)]
        + [sems(groups)],
        5 * cells,
        8 * channels * tokens,
        LIMIT,
    )(gated, value, upstream, rate_t)

    def exchange(array):
        array = array.reshape(chunks // 2, KINDS, 4, LANES)
        run = range(RUN_OF_CHIPS)
        members = [
            [2 * (late * RUN_OF_CHIPS + early) + core for early in run for late in run]
            for core in range(2)
        ]
        return lax.all_to_all(
            array, "seq", split_axis=0, concat_axis=0, axis_index_groups=members, tiled=True
        ).reshape(wire)

    states, gated_held = lax.optimization_barrier((states, gated))
    fwd, decay, gain, lam = call(
        functools.partial(ahead_kernel, modes, blocks, tokens),
        [vmem] * 4,
        [vmem] * 4,
        [signal, per_mode, per_mode, ((4, LANES), F32)],
        [one],
        4 * cells,
        6 * channels * tokens,
    )(gated_held, rate_t, residue_t, skip)
    fwd, dz = lax.optimization_barrier((fwd, dz))
    (bwd,) = call(
        functools.partial(behind_kernel, modes, blocks, tokens),
        [vmem] * 4,
        [vmem],
        [signal],
        [one],
        4 * cells,
        6 * channels * tokens,
    )(dz, decay, gain, skip)
    heard, fwd, bwd, lam = lax.optimization_barrier((exchange(states), fwd, bwd, lam))
    heard_other = lax.ppermute(heard, "seq", [(d, d ^ 1) for d in range(chunks)])
    chained = pltpu.VMEM((2,) + wire, F32)
    (entering,) = call(
        functools.partial(scan_kernel, chunks, tokens),
        [vmem] * 3,
        [vmem],
        [(wire, BF16)],
        [chained, chained],
        16 * chunks * GROUP * LANES,
        8 * chunks * GROUP * LANES,
    )(heard, heard_other, lam)
    returned = exchange(entering)
    grad_own, grad_wire = call(
        functools.partial(residue_kernel, modes, blocks),
        [vmem],
        [vmem] * 2,
        [((modes, channels), F32), ((modes, channels), BF16)],
        [unpacked, flat],
        modes * channels,
        8 * modes * channels,
    )(returned)
    grad_other = lax.ppermute(grad_wire, "ch", [(0, 1), (1, 0)]).astype(F32)
    grad_gated, grad_value, grad_res = call(
        functools.partial(final_kernel, modes, blocks, tokens),
        [vmem, vmem, hbm, vmem, vmem, hbm, vmem],
        [hbm] * 3,
        [native, native, ((modes, residue.shape[0]), F32)],
        [unpacked, [one] * groups, [one] * groups, pltpu.VMEM(*signal), raw, raw, raw]
        + [sems(groups + 2), sems(3 * groups)],
        4 * cells,
        14 * channels * tokens,
    )(returned, fwd, bwd, decay, gain, upstream, grad_own)
    place = (1 - lax.axis_index("ch")) * channels
    grad_res = lax.dynamic_update_slice(grad_res, grad_other, (0, place))
    return (grad_gated, grad_value, grad_res.T)


def solution(mesh):
    return jax.shard_map(
        local,
        mesh=mesh,
        in_specs=(P("ch", "seq"), P("ch", "seq"), P("ch", "seq"), P(), P(), P()),
        out_specs=(P("ch", "seq"), P("ch", "seq"), P()),
        check_vma=False,
    )
```

```python
import functools

import jax
import jax.numpy as jnp
from jax import lax
from jax.experimental import pallas as pl
from jax.experimental.pallas import tpu as pltpu
from jax.sharding import PartitionSpec as P

F32 = jnp.float32
BF16 = jnp.bfloat16
LANES = 128
GROUP = 8
KINDS = 3
PART, UNROLL = 8, 16
FINAL_UNROLL = 16
RUN_OF_CHIPS = 8
STATE_PART, STATE_UNROLL, RUN = 4, 32, 4
LIMIT = 56 * 2**20


def transposed(block):
    return block.astype(F32).T


def spread_modes(src_ref, dst_ref, first, modes, blocks):
    for b in range(blocks):
        start = pl.multiple_of(first + b * LANES, LANES)
        row = b // GROUP * modes * GROUP + b % GROUP
        dst_ref[pl.ds(row, modes, stride=GROUP), :] = src_ref[:, pl.ds(start, LANES)]


def tile(index):
    return pl.ds(pl.multiple_of(index * GROUP, GROUP), GROUP)


def put_signal(signal_ref, gt, b, j, tokens):
    gt[pl.ds(j, tokens, stride=GROUP), :] = transposed(signal_ref[pl.ds(b * LANES, LANES), :])


def put_dz(value_ref, upstream_ref, dz_ref, dzt, b, j, tokens):
    rows = pl.ds(b * LANES, LANES)
    dz = (upstream_ref[rows, :].astype(F32) * value_ref[rows, :].astype(F32)).astype(BF16)
    dz_ref[rows, :] = dz
    dzt[pl.ds(j, tokens, stride=GROUP), :] = transposed(dz)


def total(terms):
    while len(terms) > 1:
        pairs = [a + b for a, b in zip(terms[::2], terms[1::2])]
        terms = pairs + ([terms[-1]] if len(terms) % 2 else [])
    return terms[0]


def power(base, exponent):
    result = base
    for _ in range(exponent - 1):
        result = result * base
    return result


def horner(base, terms):
    result = terms[0]
    for term in terms[1:]:
        result = result * base + term
    return result


def state_kernel(
    modes, blocks, tokens, gated_hbm, value_hbm, upstream_hbm, rate_hbm, out_hbm, dz_hbm,
    gated_ref, value_ref, upstream_ref, dz_ref, rate_ref, gts, dzts, lam, pack, stage, sems, out_sems, dz_sems
):
    half = GROUP * LANES
    groups = blocks // GROUP
    start = pl.multiple_of(lax.axis_index("ch") * (blocks * LANES), LANES)
    rate_copy = pltpu.make_async_copy(
        rate_hbm.at[:, pl.ds(start, blocks * LANES)], rate_ref, sems.at[3 * groups]
    )
    copies = []
    for g in range(groups):
        rows = pl.ds(g * half, half)
        pairs = ((gated_hbm, gated_ref), (upstream_hbm, upstream_ref), (value_hbm, value_ref))
        copies.append(
            [
                pltpu.make_async_copy(src.at[rows, :], dst.at[rows, :], sems.at[3 * g + k])
                for k, (src, dst) in enumerate(pairs)
            ]
        )
    for copy in copies[0] + [rate_copy]:
        copy.start()
    copies[0][0].wait()
    for j in range(GROUP):
        put_signal(gated_ref, gts[0], j, j, tokens)
    copies[0][1].wait()
    copies[0][2].wait()
    for j in range(GROUP):
        put_dz(value_ref, upstream_ref, dz_ref, dzts[0], j, j, tokens)
    for part in copies[1:]:
        for copy in part:
            copy.start()
    rate_copy.wait()
    spread_modes(rate_ref, lam, 0, modes, blocks)
    zero = jnp.zeros((GROUP, LANES), F32)
    sent, late = [], []
    for g in range(groups):
        gt, dzt = gts[g], dzts[g]
        if g:
            for copy in copies[g]:
                copy.wait()
            for j in range(GROUP):
                put_signal(gated_ref, gt, g * GROUP + j, j, tokens)
                put_dz(value_ref, upstream_ref, dz_ref, dzt, g * GROUP + j, j, tokens)
        rows = pl.ds(g * half, half)
        copy = pltpu.make_async_copy(dz_ref.at[rows, :], dz_hbm.at[rows, :], dz_sems.at[g])
        copy.start()
        late.append(copy)
        lags = None
        for m0 in range(0, modes, STATE_PART):
            some = range(m0, m0 + STATE_PART)
            decay = [jnp.exp(-lam[tile(g * modes + m), :]) for m in some]
            jump = [power(a, RUN) for a in decay]

            def body(i, carry, gt=gt, dzt=dzt, decay=decay, jump=jump, first=m0 == 0):
                x, y, own, reach, lags = carry
                for u in range(STATE_UNROLL // RUN):
                    t = i * STATE_UNROLL + u * RUN
                    gs = [gt[tile(t + k), :] for k in range(RUN)]
                    ds = [dzt[tile(t + k), :] for k in range(RUN)]
                    if first:
                        lags = [
                            c + total([d * v for d, v in zip(ds[k:], gs)])
                            for k, c in enumerate(lags)
                        ]
                    ends = [horner(a, gs) for a in decay]
                    starts = [horner(a, ds[::-1]) for a in decay]
                    own = [o + v * w for o, v, w in zip(own, x, starts)]
                    y = [v + p * w for v, p, w in zip(y, reach, starts)]
                    x = [a * v + w for a, v, w in zip(jump, x, ends)]
                    reach = [a * p for a, p in zip(jump, reach)]
                return x, y, own, reach, lags

            zeros = [zero] * STATE_PART
            ones = [zero + 1.0] * STATE_PART
            carry = (zeros, zeros, zeros, ones, [zero] * RUN if m0 == 0 else [])
            x, y, own, _, found = lax.fori_loop(0, tokens // STATE_UNROLL, body, carry)
            lags = found if m0 == 0 else lags
            for k in range(STATE_PART):
                base = (m0 + k) * GROUP * 2 * KINDS + g * KINDS
                term = decay[k] * own[k] + horner(decay[k], lags[::-1])
                for kind, rows in enumerate((x[k], y[k], term)):
                    pack[pl.ds(base + kind, GROUP, stride=2 * KINDS), :] = rows
            if g < groups - 1:
                continue
            rows = pl.ds(m0 * GROUP * 2 * KINDS, STATE_PART * GROUP * 2 * KINDS)
            stage[rows, :] = pack[rows, :].astype(BF16)
            copy = pltpu.make_async_copy(
                stage.at[rows, :], out_hbm.at[rows, :], out_sems.at[len(sent)]
            )
            copy.start()
            sent.append(copy)
    for copy in sent + late:
        copy.wait()


def own_sums(modes, tokens, g, signal, out_ref, dec_ref, gain_ref, skip, order):
    zero = jnp.zeros((GROUP, LANES), F32)
    for m0 in range(0, modes, PART):
        decay = [dec_ref[tile(g * modes + m), :] for m in range(m0, m0 + PART)]
        gain = [gain_ref[tile(g * modes + m), :] for m in range(m0, m0 + PART)]

        def body(i, x, m0=m0, decay=decay, gain=gain):
            for u in range(UNROLL):
                t = order(i * UNROLL + u)
                at = tile(g * tokens + t)
                v = signal[tile(t), :]
                x = [a * w + v for a, w in zip(decay, x)]
                known = out_ref[at, :] if m0 else skip * v
                out_ref[at, :] = total([r * w for r, w in zip(gain, x)] + [known])
            return x

        lax.fori_loop(0, tokens // UNROLL, body, [zero] * PART)


def skip_of(skip_ref, first, g):
    parts = [
        skip_ref[:, pl.ds(pl.multiple_of(first + (g * GROUP + j) * LANES, LANES), LANES)]
        for j in range(GROUP)
    ]
    return jnp.concatenate(parts, axis=0)


def place_of(chip):
    z = chip % RUN_OF_CHIPS
    return (z % 4 * 2 + z // 4) * RUN_OF_CHIPS + chip // RUN_OF_CHIPS


def ahead_kernel(
    modes, blocks, tokens, gated_ref, rate_ref, res_ref, skip_ref,
    fwd_ref, dec_ref, gain_ref, lam_ref, gt
):
    first = lax.axis_index("ch") * (blocks * LANES)
    spread_modes(rate_ref, dec_ref, first, modes, blocks)
    spread_modes(res_ref, gain_ref, first, modes, blocks)
    for h in range(2):
        for g in range(blocks // GROUP):
            chip = lax.axis_index("seq") // 2
            row = g * modes * GROUP + place_of(chip) * 2 + h
            own = dec_ref[pl.ds(row, 1), :]
            lam_ref[pl.ds(2 * h + g, 1), :] = own
    dec_ref[...] = jnp.exp(-dec_ref[...])
    for g in range(blocks // GROUP):
        for j in range(GROUP):
            put_signal(gated_ref, gt, g * GROUP + j, j, tokens)
        skip = skip_of(skip_ref, first, g)
        own_sums(modes, tokens, g, gt, fwd_ref, dec_ref, gain_ref, skip, lambda t: t)


def behind_kernel(modes, blocks, tokens, dz_ref, dec_ref, gain_ref, skip_ref, bwd_ref, dzt):
    first = lax.axis_index("ch") * (blocks * LANES)
    for g in range(blocks // GROUP):
        for j in range(GROUP):
            put_signal(dz_ref, dzt, g * GROUP + j, j, tokens)
        skip = skip_of(skip_ref, first, g)
        order = lambda t: tokens - 1 - t
        own_sums(modes, tokens, g, dzt, bwd_ref, dec_ref, gain_ref, skip, order)


def scan_kernel(chunks, tokens, own_ref, other_ref, lam_ref, out_ref, sums, outs):
    core = lax.axis_index("seq") % 2
    chips = chunks // 2
    sums[core] = own_ref[...].astype(F32)
    sums[1 - core] = other_ref[...].astype(F32)
    lam = lam_ref[...]
    step = jnp.exp(lam * (-1.0 * tokens))
    zero = jnp.zeros((4, LANES), F32)

    def at(q, kind):
        return pl.ds(q * 4 * KINDS + kind, 4, stride=KINDS)

    def body(i, carry):
        x, y, own, cross = carry
        for u in range(RUN_OF_CHIPS):
            q = place_of(u) + i
            r = place_of(RUN_OF_CHIPS - 1 - u) + RUN_OF_CHIPS - 1 - i
            for place in range(2):
                outs[place, at(q, 0), :] = x
                outs[1 - place, at(r, 1), :] = y
                own = own + sums[place, at(q, 2), :]
                cross = cross + sums[place, at(q, 1), :] * x
                x = step * x + sums[place, at(q, 0), :]
                y = step * y + sums[1 - place, at(r, 1), :]
        return x, y, own, cross

    _, _, own, cross = lax.fori_loop(0, RUN_OF_CHIPS, body, (zero, zero, zero, zero))
    grad = (own + cross * jnp.exp(-lam)) * (1.0 / (chunks * tokens))
    for q in range(chips):
        outs[core, at(q, 2), :] = grad
    out_ref[...] = outs[core].astype(BF16)


def residue_kernel(modes, blocks, in_ref, out_ref, wire_ref, tiles, flat):
    tiles[...] = in_ref[...].astype(F32)
    for r in range(modes * blocks // GROUP):
        base = r % modes * GROUP * 2 * KINDS + r // modes * KINDS
        flat[pl.ds(r * GROUP, GROUP), :] = tiles[pl.ds(base + 2, GROUP, stride=2 * KINDS), :]
    for b in range(blocks):
        row = b // GROUP * modes * GROUP + b % GROUP
        found = flat[pl.ds(row, modes, stride=GROUP), :]
        out_ref[:, pl.ds(b * LANES, LANES)] = found
        wire_ref[:, pl.ds(b * LANES, LANES)] = found.astype(BF16)


def final_kernel(
    modes, blocks, tokens, in_ref, fwd_ref, bwd_hbm, dec_ref, gain_ref, upstream_hbm, residue_ref,
    grad_gated_hbm, grad_value_hbm, grad_residue_hbm, tiles, zts, gts, bwd_ref, upstream_ref, grad_gated_ref,
    grad_value_ref, in_sems, sems
):
    groups = blocks // GROUP
    half = GROUP * LANES
    own_copies = []
    for g in range(groups):
        rows = pl.ds(g * tokens * GROUP, tokens * GROUP)
        own_copies.append(
            pltpu.make_async_copy(bwd_hbm.at[rows, :], bwd_ref.at[rows, :], in_sems.at[g])
        )
    upstream_copy = pltpu.make_async_copy(upstream_hbm, upstream_ref, in_sems.at[groups])
    channels = blocks * LANES
    start = pl.multiple_of(lax.axis_index("ch") * channels, LANES)
    residue_copy = pltpu.make_async_copy(
        residue_ref, grad_residue_hbm.at[:, pl.ds(start, channels)], in_sems.at[groups + 1]
    )
    for copy in [own_copies[0], upstream_copy] + own_copies[1:] + [residue_copy]:
        copy.start()
    tiles[...] = in_ref[...].astype(F32)
    copies = []

    def send(src, dst, first, size):
        rows = pl.ds(first * LANES, size * LANES)
        copy = pltpu.make_async_copy(src.at[rows, :], dst.at[rows, :], sems.at[len(copies)])
        copy.start()
        copies.append(copy)

    for g in range(groups):
        decay = [dec_ref[tile(g * modes + m), :] for m in range(modes)]
        scale = [gain_ref[tile(g * modes + m), :] * decay[m] for m in range(modes)]

        def entering(kind, g=g, scale=scale):
            bases = [m * GROUP * 2 * KINDS + g * KINDS + kind for m in range(modes)]
            return [
                tiles[pl.ds(base, GROUP, stride=2 * KINDS), :] * a for base, a in zip(bases, scale)
            ]

        def ahead(i, x, g=g, decay=decay):
            for u in range(FINAL_UNROLL):
                t = i * FINAL_UNROLL + u
                zts[g][tile(t), :] = fwd_ref[tile(g * tokens + t), :] + total(list(x))
                x = [a * v for a, v in zip(decay, x)]
            return x

        def behind(i, y, g=g, decay=decay):
            for u in range(FINAL_UNROLL):
                s = tokens - 1 - i * FINAL_UNROLL - u
                gts[g][tile(s), :] = bwd_ref[tile(g * tokens + s), :] + total(list(y))
                y = [a * v for a, v in zip(decay, y)]
            return y

        lax.fori_loop(0, tokens // FINAL_UNROLL, ahead, entering(0))
        if g == 0:
            upstream_copy.wait()
        for j in range(GROUP):
            rows = pl.ds(g * half + j * LANES, LANES)
            z = transposed(zts[g][pl.ds(j, tokens, stride=GROUP), :].astype(BF16))
            grad_value_ref[rows, :] = (upstream_ref[rows, :].astype(F32) * z).astype(BF16)
        send(grad_value_ref, grad_value_hbm, g * GROUP, GROUP)
        own_copies[g].wait()
        lax.fori_loop(0, tokens // FINAL_UNROLL, behind, entering(1))
        for j in range(GROUP):
            rows = pl.ds(g * half + j * LANES, LANES)
            back = transposed(gts[g][pl.ds(j, tokens, stride=GROUP), :].astype(BF16))
            grad_gated_ref[rows, :] = back.astype(BF16)
            if j % 4 == 3:
                send(grad_gated_ref, grad_gated_hbm, g * GROUP + j - 3, 4)
    for copy in copies + [residue_copy]:
        copy.wait()


def local(gated, value, upstream, residue, rate, skip_weight):
    channels, tokens = gated.shape
    modes = rate.shape[1]
    chunks = lax.axis_size("seq")
    blocks = channels // LANES
    pairs = modes * blocks
    groups = blocks // GROUP
    assert tokens == LANES == UNROLL * GROUP and pairs == 2 * chunks
    assert blocks == 2 * GROUP and modes == 2 * PART and chunks == 2 * RUN_OF_CHIPS**2
    rate_t, residue_t, skip = rate.T, residue.T, skip_weight[None, :]
    vmem = pl.BlockSpec(memory_space=pltpu.VMEM)
    hbm = pl.BlockSpec(memory_space=pltpu.HBM)
    cells = modes * channels * tokens

    def call(kernel, specs, out_specs, shapes, scratch, flops, size, limit=16 * 2**20):
        return pl.pallas_call(
            kernel,
            in_specs=specs,
            out_specs=out_specs,
            out_shape=[jax.ShapeDtypeStruct(*shape) for shape in shapes],
            scratch_shapes=scratch,
            compiler_params=pltpu.CompilerParams(vmem_limit_bytes=limit),
            cost_estimate=pl.CostEstimate(flops=flops, bytes_accessed=size, transcendentals=0),
        )

    native = ((channels, tokens), BF16)
    signal = ((tokens * blocks, LANES), F32)
    per_mode = ((pairs, LANES), F32)
    wire = (chunks * 2 * KINDS, LANES)
    one = pltpu.VMEM((tokens * GROUP, LANES), F32)
    raw = pltpu.VMEM(*native)
    unpacked = pltpu.VMEM(wire, F32)
    staged = pltpu.VMEM(wire, BF16)
    flat = pltpu.VMEM(*per_mode)
    sems = lambda count: pltpu.SemaphoreType.DMA((count,))
    states, dz = call(
        functools.partial(state_kernel, modes, blocks, tokens),
        [hbm] * 4,
        [hbm] * 2,
        [(wire, BF16), native],
        [raw, raw, raw, raw, pltpu.VMEM((modes, channels), F32), [one] * groups, [one] * groups]
        + [flat, unpacked, staged, sems(3 * groups + 1), sems(modes // STATE_PART)]
        + [sems(groups)],
        5 * cells,
        8 * channels * tokens,
        LIMIT,
    )(gated, value, upstream, rate_t)

    def exchange(array):
        array = array.reshape(chunks // 2, KINDS, 4, LANES)
        by_place = sorted(range(chunks // 2), key=place_of)
        members = [[2 * chip + core for chip in by_place] for core in range(2)]
        return lax.all_to_all(
            array, "seq", split_axis=0, concat_axis=0, axis_index_groups=members, tiled=True
        ).reshape(wire)

    states, gated_held = lax.optimization_barrier((states, gated))
    fwd, decay, gain, lam = call(
        functools.partial(ahead_kernel, modes, blocks, tokens),
        [vmem] * 4,
        [vmem] * 4,
        [signal, per_mode, per_mode, ((4, LANES), F32)],
        [one],
        4 * cells,
        6 * channels * tokens,
    )(gated_held, rate_t, residue_t, skip)
    fwd, dz = lax.optimization_barrier((fwd, dz))
    (bwd,) = call(
        functools.partial(behind_kernel, modes, blocks, tokens),
        [vmem] * 4,
        [vmem],
        [signal],
        [one],
        4 * cells,
        6 * channels * tokens,
    )(dz, decay, gain, skip)
    heard, fwd, bwd, lam = lax.optimization_barrier((exchange(states), fwd, bwd, lam))
    heard_other = lax.ppermute(heard, "seq", [(d, d ^ 1) for d in range(chunks)])
    chained = pltpu.VMEM((2,) + wire, F32)
    (entering,) = call(
        functools.partial(scan_kernel, chunks, tokens),
        [vmem] * 3,
        [vmem],
        [(wire, BF16)],
        [chained, chained],
        16 * chunks * GROUP * LANES,
        8 * chunks * GROUP * LANES,
    )(heard, heard_other, lam)
    returned = exchange(entering)
    grad_own, grad_wire = call(
        functools.partial(residue_kernel, modes, blocks),
        [vmem],
        [vmem] * 2,
        [((modes, channels), F32), ((modes, channels), BF16)],
        [unpacked, flat],
        modes * channels,
        8 * modes * channels,
    )(returned)
    grad_other = lax.ppermute(grad_wire, "ch", [(0, 1), (1, 0)]).astype(F32)
    grad_gated, grad_value, grad_res = call(
        functools.partial(final_kernel, modes, blocks, tokens),
        [vmem, vmem, hbm, vmem, vmem, hbm, vmem],
        [hbm] * 3,
        [native, native, ((modes, residue.shape[0]), F32)],
        [unpacked, [one] * groups, [one] * groups, pltpu.VMEM(*signal), raw, raw, raw]
        + [sems(groups + 2), sems(3 * groups)],
        4 * cells,
        14 * channels * tokens,
    )(returned, fwd, bwd, decay, gain, upstream, grad_own)
    place = (1 - lax.axis_index("ch")) * channels
    grad_res = lax.dynamic_update_slice(grad_res, grad_other, (0, place))
    return (grad_gated, grad_value, grad_res.T)


def solution(mesh):
    return jax.shard_map(
        local,
        mesh=mesh,
        in_specs=(P("ch", "seq"), P("ch", "seq"), P("ch", "seq"), P(), P(), P()),
        out_specs=(P("ch", "seq"), P("ch", "seq"), P()),
        check_vma=False,
    )
```

```python
import functools

import jax
import jax.numpy as jnp
from jax import lax
from jax.experimental import pallas as pl
from jax.experimental.pallas import tpu as pltpu
from jax.sharding import PartitionSpec as P

F32 = jnp.float32
BF16 = jnp.bfloat16
LANES = 128
GROUP = 8
KINDS = 3
PART, UNROLL = 8, 16
FINAL_UNROLL = 16
RUN_OF_CHIPS = 8
STATE_PART, STATE_UNROLL, RUN = 4, 64, 4
LIMIT = 56 * 2**20


def transposed(block):
    return block.astype(F32).T


def spread_modes(src_ref, dst_ref, first, modes, blocks):
    for b in range(blocks):
        start = pl.multiple_of(first + b * LANES, LANES)
        row = b // GROUP * modes * GROUP + b % GROUP
        dst_ref[pl.ds(row, modes, stride=GROUP), :] = src_ref[:, pl.ds(start, LANES)]


def tile(index):
    return pl.ds(pl.multiple_of(index * GROUP, GROUP), GROUP)


def put_signal(signal_ref, gt, b, j, tokens):
    gt[pl.ds(j, tokens, stride=GROUP), :] = transposed(signal_ref[pl.ds(b * LANES, LANES), :])


def put_dz(value_ref, upstream_ref, dz_ref, dzt, b, j, tokens):
    rows = pl.ds(b * LANES, LANES)
    dz = (upstream_ref[rows, :].astype(F32) * value_ref[rows, :].astype(F32)).astype(BF16)
    dz_ref[rows, :] = dz
    dzt[pl.ds(j, tokens, stride=GROUP), :] = transposed(dz)


def total(terms):
    while len(terms) > 1:
        pairs = [a + b for a, b in zip(terms[::2], terms[1::2])]
        terms = pairs + ([terms[-1]] if len(terms) % 2 else [])
    return terms[0]


def power(base, exponent):
    result = base
    for _ in range(exponent - 1):
        result = result * base
    return result


def horner(base, terms):
    result = terms[0]
    for term in terms[1:]:
        result = result * base + term
    return result


def state_kernel(
    modes, blocks, tokens, gated_hbm, value_hbm, upstream_hbm, rate_hbm, out_hbm, dz_hbm,
    gated_ref, value_ref, upstream_ref, dz_ref, rate_ref, gts, dzts, lam, pack, stage, sems, out_sems, dz_sems
):
    half = GROUP * LANES
    groups = blocks // GROUP
    start = pl.multiple_of(lax.axis_index("ch") * (blocks * LANES), LANES)
    rate_copy = pltpu.make_async_copy(
        rate_hbm.at[:, pl.ds(start, blocks * LANES)], rate_ref, sems.at[3 * groups]
    )
    copies = []
    for g in range(groups):
        rows = pl.ds(g * half, half)
        pairs = ((gated_hbm, gated_ref), (upstream_hbm, upstream_ref), (value_hbm, value_ref))
        copies.append(
            [
                pltpu.make_async_copy(src.at[rows, :], dst.at[rows, :], sems.at[3 * g + k])
                for k, (src, dst) in enumerate(pairs)
            ]
        )
    for copy in copies[0] + [rate_copy]:
        copy.start()
    copies[0][0].wait()
    for j in range(GROUP):
        put_signal(gated_ref, gts[0], j, j, tokens)
    copies[0][1].wait()
    copies[0][2].wait()
    for j in range(GROUP):
        put_dz(value_ref, upstream_ref, dz_ref, dzts[0], j, j, tokens)
    for part in copies[1:]:
        for copy in part:
            copy.start()
    rate_copy.wait()
    spread_modes(rate_ref, lam, 0, modes, blocks)
    zero = jnp.zeros((GROUP, LANES), F32)
    sent, late = [], []
    for g in range(groups):
        gt, dzt = gts[g], dzts[g]
        if g:
            for copy in copies[g]:
                copy.wait()
            for j in range(GROUP):
                put_signal(gated_ref, gt, g * GROUP + j, j, tokens)
                put_dz(value_ref, upstream_ref, dz_ref, dzt, g * GROUP + j, j, tokens)
        rows = pl.ds(g * half, half)
        copy = pltpu.make_async_copy(dz_ref.at[rows, :], dz_hbm.at[rows, :], dz_sems.at[g])
        copy.start()
        late.append(copy)
        lags = None
        for m0 in range(0, modes, STATE_PART):
            some = range(m0, m0 + STATE_PART)
            decay = [jnp.exp(-lam[tile(g * modes + m), :]) for m in some]
            jump = [power(a, RUN) for a in decay]

            def body(i, carry, gt=gt, dzt=dzt, decay=decay, jump=jump, first=m0 == 0):
                x, y, own, reach, lags = carry
                for u in range(STATE_UNROLL // RUN):
                    t = i * STATE_UNROLL + u * RUN
                    gs = [gt[tile(t + k), :] for k in range(RUN)]
                    ds = [dzt[tile(t + k), :] for k in range(RUN)]
                    if first:
                        lags = [
                            c + total([d * v for d, v in zip(ds[k:], gs)])
                            for k, c in enumerate(lags)
                        ]
                    ends = [horner(a, gs) for a in decay]
                    starts = [horner(a, ds[::-1]) for a in decay]
                    own = [o + v * w for o, v, w in zip(own, x, starts)]
                    y = [v + p * w for v, p, w in zip(y, reach, starts)]
                    x = [a * v + w for a, v, w in zip(jump, x, ends)]
                    reach = [a * p for a, p in zip(jump, reach)]
                return x, y, own, reach, lags

            zeros = [zero] * STATE_PART
            ones = [zero + 1.0] * STATE_PART
            carry = (zeros, zeros, zeros, ones, [zero] * RUN if m0 == 0 else [])
            x, y, own, _, found = lax.fori_loop(0, tokens // STATE_UNROLL, body, carry)
            lags = found if m0 == 0 else lags
            for k in range(STATE_PART):
                base = (m0 + k) * GROUP * 2 * KINDS + g * KINDS
                term = decay[k] * own[k] + horner(decay[k], lags[::-1])
                for kind, rows in enumerate((x[k], y[k], term)):
                    pack[pl.ds(base + kind, GROUP, stride=2 * KINDS), :] = rows
            if g < groups - 1:
                continue
            rows = pl.ds(m0 * GROUP * 2 * KINDS, STATE_PART * GROUP * 2 * KINDS)
            stage[rows, :] = pack[rows, :].astype(BF16)
            copy = pltpu.make_async_copy(
                stage.at[rows, :], out_hbm.at[rows, :], out_sems.at[len(sent)]
            )
            copy.start()
            sent.append(copy)
    for copy in sent + late:
        copy.wait()


def own_sums(modes, tokens, g, signal, out_ref, dec_ref, gain_ref, skip, order):
    zero = jnp.zeros((GROUP, LANES), F32)
    for m0 in range(0, modes, PART):
        decay = [dec_ref[tile(g * modes + m), :] for m in range(m0, m0 + PART)]
        gain = [gain_ref[tile(g * modes + m), :] for m in range(m0, m0 + PART)]

        def body(i, x, m0=m0, decay=decay, gain=gain):
            for u in range(UNROLL):
                t = order(i * UNROLL + u)
                at = tile(g * tokens + t)
                v = signal[tile(t), :]
                x = [a * w + v for a, w in zip(decay, x)]
                known = out_ref[at, :] if m0 else skip * v
                out_ref[at, :] = total([r * w for r, w in zip(gain, x)] + [known])
            return x

        lax.fori_loop(0, tokens // UNROLL, body, [zero] * PART)


def skip_of(skip_ref, first, g):
    parts = [
        skip_ref[:, pl.ds(pl.multiple_of(first + (g * GROUP + j) * LANES, LANES), LANES)]
        for j in range(GROUP)
    ]
    return jnp.concatenate(parts, axis=0)


def place_of(chip):
    z = chip % RUN_OF_CHIPS
    return (z % 4 * 2 + z // 4) * RUN_OF_CHIPS + chip // RUN_OF_CHIPS


def ahead_kernel(
    modes, blocks, tokens, gated_ref, rate_ref, res_ref, skip_ref,
    fwd_ref, dec_ref, gain_ref, lam_ref, gt
):
    first = lax.axis_index("ch") * (blocks * LANES)
    spread_modes(rate_ref, dec_ref, first, modes, blocks)
    spread_modes(res_ref, gain_ref, first, modes, blocks)
    for h in range(2):
        for g in range(blocks // GROUP):
            chip = lax.axis_index("seq") // 2
            row = g * modes * GROUP + place_of(chip) * 2 + h
            own = dec_ref[pl.ds(row, 1), :]
            lam_ref[pl.ds(2 * h + g, 1), :] = own
    dec_ref[...] = jnp.exp(-dec_ref[...])
    for g in range(blocks // GROUP):
        for j in range(GROUP):
            put_signal(gated_ref, gt, g * GROUP + j, j, tokens)
        skip = skip_of(skip_ref, first, g)
        own_sums(modes, tokens, g, gt, fwd_ref, dec_ref, gain_ref, skip, lambda t: t)


def behind_kernel(modes, blocks, tokens, dz_ref, dec_ref, gain_ref, skip_ref, bwd_ref, dzt):
    first = lax.axis_index("ch") * (blocks * LANES)
    for g in range(blocks // GROUP):
        for j in range(GROUP):
            put_signal(dz_ref, dzt, g * GROUP + j, j, tokens)
        skip = skip_of(skip_ref, first, g)
        order = lambda t: tokens - 1 - t
        own_sums(modes, tokens, g, dzt, bwd_ref, dec_ref, gain_ref, skip, order)


def scan_kernel(chunks, tokens, own_ref, other_ref, lam_ref, out_ref, sums, outs):
    core = lax.axis_index("seq") % 2
    chips = chunks // 2
    sums[core] = own_ref[...].astype(F32)
    sums[1 - core] = other_ref[...].astype(F32)
    lam = lam_ref[...]
    step = jnp.exp(lam * (-1.0 * tokens))
    zero = jnp.zeros((4, LANES), F32)

    def at(q, kind):
        return pl.ds(q * 4 * KINDS + kind, 4, stride=KINDS)

    def body(i, carry):
        x, y, own, cross = carry
        for u in range(RUN_OF_CHIPS):
            q = place_of(u) + i
            r = place_of(RUN_OF_CHIPS - 1 - u) + RUN_OF_CHIPS - 1 - i
            for place in range(2):
                outs[place, at(q, 0), :] = x
                outs[1 - place, at(r, 1), :] = y
                own = own + sums[place, at(q, 2), :]
                cross = cross + sums[place, at(q, 1), :] * x
                x = step * x + sums[place, at(q, 0), :]
                y = step * y + sums[1 - place, at(r, 1), :]
        return x, y, own, cross

    _, _, own, cross = lax.fori_loop(0, RUN_OF_CHIPS, body, (zero, zero, zero, zero))
    grad = (own + cross * jnp.exp(-lam)) * (1.0 / (chunks * tokens))
    for q in range(chips):
        outs[core, at(q, 2), :] = grad
    out_ref[...] = outs[core].astype(BF16)


def residue_kernel(modes, blocks, in_ref, out_ref, wire_ref, tiles, flat):
    tiles[...] = in_ref[...].astype(F32)
    for r in range(modes * blocks // GROUP):
        base = r % modes * GROUP * 2 * KINDS + r // modes * KINDS
        flat[pl.ds(r * GROUP, GROUP), :] = tiles[pl.ds(base + 2, GROUP, stride=2 * KINDS), :]
    for b in range(blocks):
        row = b // GROUP * modes * GROUP + b % GROUP
        found = flat[pl.ds(row, modes, stride=GROUP), :]
        out_ref[:, pl.ds(b * LANES, LANES)] = found
        wire_ref[:, pl.ds(b * LANES, LANES)] = found.astype(BF16)


def final_kernel(
    modes, blocks, tokens, in_ref, fwd_ref, bwd_hbm, dec_ref, gain_ref, upstream_hbm, residue_ref,
    grad_gated_hbm, grad_value_hbm, grad_residue_hbm, tiles, zts, gts, bwd_ref, upstream_ref, grad_gated_ref,
    grad_value_ref, in_sems, sems
):
    groups = blocks // GROUP
    half = GROUP * LANES
    own_copies = []
    for g in range(groups):
        rows = pl.ds(g * tokens * GROUP, tokens * GROUP)
        own_copies.append(
            pltpu.make_async_copy(bwd_hbm.at[rows, :], bwd_ref.at[rows, :], in_sems.at[g])
        )
    upstream_copy = pltpu.make_async_copy(upstream_hbm, upstream_ref, in_sems.at[groups])
    channels = blocks * LANES
    start = pl.multiple_of(lax.axis_index("ch") * channels, LANES)
    residue_copy = pltpu.make_async_copy(
        residue_ref, grad_residue_hbm.at[:, pl.ds(start, channels)], in_sems.at[groups + 1]
    )
    for copy in [own_copies[0], upstream_copy] + own_copies[1:] + [residue_copy]:
        copy.start()
    tiles[...] = in_ref[...].astype(F32)
    copies = []

    def send(src, dst, first, size):
        rows = pl.ds(first * LANES, size * LANES)
        copy = pltpu.make_async_copy(src.at[rows, :], dst.at[rows, :], sems.at[len(copies)])
        copy.start()
        copies.append(copy)

    for g in range(groups):
        decay = [dec_ref[tile(g * modes + m), :] for m in range(modes)]
        scale = [gain_ref[tile(g * modes + m), :] * decay[m] for m in range(modes)]

        def entering(kind, g=g, scale=scale):
            bases = [m * GROUP * 2 * KINDS + g * KINDS + kind for m in range(modes)]
            return [
                tiles[pl.ds(base, GROUP, stride=2 * KINDS), :] * a for base, a in zip(bases, scale)
            ]

        def ahead(i, x, g=g, decay=decay):
            for u in range(FINAL_UNROLL):
                t = i * FINAL_UNROLL + u
                zts[g][tile(t), :] = fwd_ref[tile(g * tokens + t), :] + total(list(x))
                x = [a * v for a, v in zip(decay, x)]
            return x

        def behind(i, y, g=g, decay=decay):
            for u in range(FINAL_UNROLL):
                s = tokens - 1 - i * FINAL_UNROLL - u
                gts[g][tile(s), :] = bwd_ref[tile(g * tokens + s), :] + total(list(y))
                y = [a * v for a, v in zip(decay, y)]
            return y

        lax.fori_loop(0, tokens // FINAL_UNROLL, ahead, entering(0))
        if g == 0:
            upstream_copy.wait()
        for j in range(GROUP):
            rows = pl.ds(g * half + j * LANES, LANES)
            z = transposed(zts[g][pl.ds(j, tokens, stride=GROUP), :].astype(BF16))
            grad_value_ref[rows, :] = (upstream_ref[rows, :].astype(F32) * z).astype(BF16)
        send(grad_value_ref, grad_value_hbm, g * GROUP, GROUP)
        own_copies[g].wait()
        lax.fori_loop(0, tokens // FINAL_UNROLL, behind, entering(1))
        for j in range(GROUP):
            rows = pl.ds(g * half + j * LANES, LANES)
            back = transposed(gts[g][pl.ds(j, tokens, stride=GROUP), :].astype(BF16))
            grad_gated_ref[rows, :] = back.astype(BF16)
            if j == 3:
                send(grad_gated_ref, grad_gated_hbm, g * GROUP, 4)
            elif j in (5, 7):
                send(grad_gated_ref, grad_gated_hbm, g * GROUP + j - 1, 2)
    for copy in copies + [residue_copy]:
        copy.wait()


def local(gated, value, upstream, residue, rate, skip_weight):
    channels, tokens = gated.shape
    modes = rate.shape[1]
    chunks = lax.axis_size("seq")
    blocks = channels // LANES
    pairs = modes * blocks
    groups = blocks // GROUP
    assert tokens == LANES == UNROLL * GROUP and pairs == 2 * chunks
    assert blocks == 2 * GROUP and modes == 2 * PART and chunks == 2 * RUN_OF_CHIPS**2
    rate_t, residue_t, skip = rate.T, residue.T, skip_weight[None, :]
    vmem = pl.BlockSpec(memory_space=pltpu.VMEM)
    hbm = pl.BlockSpec(memory_space=pltpu.HBM)
    cells = modes * channels * tokens

    def call(kernel, specs, out_specs, shapes, scratch, flops, size, limit=16 * 2**20):
        return pl.pallas_call(
            kernel,
            in_specs=specs,
            out_specs=out_specs,
            out_shape=[jax.ShapeDtypeStruct(*shape) for shape in shapes],
            scratch_shapes=scratch,
            compiler_params=pltpu.CompilerParams(vmem_limit_bytes=limit),
            cost_estimate=pl.CostEstimate(flops=flops, bytes_accessed=size, transcendentals=0),
        )

    native = ((channels, tokens), BF16)
    signal = ((tokens * blocks, LANES), F32)
    per_mode = ((pairs, LANES), F32)
    wire = (chunks * 2 * KINDS, LANES)
    one = pltpu.VMEM((tokens * GROUP, LANES), F32)
    raw = pltpu.VMEM(*native)
    unpacked = pltpu.VMEM(wire, F32)
    staged = pltpu.VMEM(wire, BF16)
    flat = pltpu.VMEM(*per_mode)
    sems = lambda count: pltpu.SemaphoreType.DMA((count,))
    states, dz = call(
        functools.partial(state_kernel, modes, blocks, tokens),
        [hbm] * 4,
        [hbm] * 2,
        [(wire, BF16), native],
        [raw, raw, raw, raw, pltpu.VMEM((modes, channels), F32), [one] * groups, [one] * groups]
        + [flat, unpacked, staged, sems(3 * groups + 1), sems(modes // STATE_PART)]
        + [sems(groups)],
        5 * cells,
        8 * channels * tokens,
        LIMIT,
    )(gated, value, upstream, rate_t)

    def exchange(array):
        array = array.reshape(chunks // 2, KINDS, 4, LANES)
        by_place = sorted(range(chunks // 2), key=place_of)
        members = [[2 * chip + core for chip in by_place] for core in range(2)]
        return lax.all_to_all(
            array, "seq", split_axis=0, concat_axis=0, axis_index_groups=members, tiled=True
        ).reshape(wire)

    states, gated_held = lax.optimization_barrier((states, gated))
    fwd, decay, gain, lam = call(
        functools.partial(ahead_kernel, modes, blocks, tokens),
        [vmem] * 4,
        [vmem] * 4,
        [signal, per_mode, per_mode, ((4, LANES), F32)],
        [one],
        4 * cells,
        6 * channels * tokens,
    )(gated_held, rate_t, residue_t, skip)
    fwd, dz = lax.optimization_barrier((fwd, dz))
    (bwd,) = call(
        functools.partial(behind_kernel, modes, blocks, tokens),
        [vmem] * 4,
        [vmem],
        [signal],
        [one],
        4 * cells,
        6 * channels * tokens,
    )(dz, decay, gain, skip)
    heard, fwd, bwd, lam = lax.optimization_barrier((exchange(states), fwd, bwd, lam))
    heard_other = lax.ppermute(heard, "seq", [(d, d ^ 1) for d in range(chunks)])
    chained = pltpu.VMEM((2,) + wire, F32)
    (entering,) = call(
        functools.partial(scan_kernel, chunks, tokens),
        [vmem] * 3,
        [vmem],
        [(wire, BF16)],
        [chained, chained],
        16 * chunks * GROUP * LANES,
        8 * chunks * GROUP * LANES,
    )(heard, heard_other, lam)
    returned = exchange(entering)
    grad_own, grad_wire = call(
        functools.partial(residue_kernel, modes, blocks),
        [vmem],
        [vmem] * 2,
        [((modes, channels), F32), ((modes, channels), BF16)],
        [unpacked, flat],
        modes * channels,
        8 * modes * channels,
    )(returned)
    grad_other = lax.ppermute(grad_wire, "ch", [(0, 1), (1, 0)]).astype(F32)
    grad_gated, grad_value, grad_res = call(
        functools.partial(final_kernel, modes, blocks, tokens),
        [vmem, vmem, hbm, vmem, vmem, hbm, vmem],
        [hbm] * 3,
        [native, native, ((modes, residue.shape[0]), F32)],
        [unpacked, [one] * groups, [one] * groups, pltpu.VMEM(*signal), raw, raw, raw]
        + [sems(groups + 2), sems(4 * groups)],
        4 * cells,
        14 * channels * tokens,
    )(returned, fwd, bwd, decay, gain, upstream, grad_own)
    place = (1 - lax.axis_index("ch")) * channels
    grad_res = lax.dynamic_update_slice(grad_res, grad_other, (0, place))
    return (grad_gated, grad_value, grad_res.T)


def solution(mesh):
    return jax.shard_map(
        local,
        mesh=mesh,
        in_specs=(P("ch", "seq"), P("ch", "seq"), P("ch", "seq"), P(), P(), P()),
        out_specs=(P("ch", "seq"), P("ch", "seq"), P()),
        check_vma=False,
    )
```

```python
import functools

import jax
import jax.numpy as jnp
from jax import lax
from jax.experimental import pallas as pl
from jax.experimental.pallas import tpu as pltpu
from jax.sharding import PartitionSpec as P

F32 = jnp.float32
BF16 = jnp.bfloat16
LANES = 128
GROUP = 8
KINDS = 3
PART, UNROLL = 8, 16
FINAL_UNROLL = 16
RUN_OF_CHIPS = 8
STATE_PART, STATE_UNROLL, RUN = 4, 64, 4
LIMIT = 56 * 2**20


def transposed(block):
    return block.astype(F32).T


def spread_modes(src_ref, dst_ref, first, modes, blocks):
    for b in range(blocks):
        start = pl.multiple_of(first + b * LANES, LANES)
        row = b // GROUP * modes * GROUP + b % GROUP
        dst_ref[pl.ds(row, modes, stride=GROUP), :] = src_ref[:, pl.ds(start, LANES)]


def tile(index):
    return pl.ds(pl.multiple_of(index * GROUP, GROUP), GROUP)


def put_signal(signal_ref, gt, b, j, tokens):
    gt[pl.ds(j, tokens, stride=GROUP), :] = transposed(signal_ref[pl.ds(b * LANES, LANES), :])


def put_dz(value_ref, upstream_ref, dz_ref, dzt, b, j, tokens):
    rows = pl.ds(b * LANES, LANES)
    dz = (upstream_ref[rows, :].astype(F32) * value_ref[rows, :].astype(F32)).astype(BF16)
    dz_ref[rows, :] = dz
    dzt[pl.ds(j, tokens, stride=GROUP), :] = transposed(dz)


def total(terms):
    while len(terms) > 1:
        pairs = [a + b for a, b in zip(terms[::2], terms[1::2])]
        terms = pairs + ([terms[-1]] if len(terms) % 2 else [])
    return terms[0]


def power(base, exponent):
    result = base
    for _ in range(exponent - 1):
        result = result * base
    return result


def horner(base, terms):
    result = terms[0]
    for term in terms[1:]:
        result = result * base + term
    return result


def state_kernel(
    modes, blocks, tokens, gated_hbm, value_hbm, upstream_hbm, rate_hbm, out_hbm, dz_hbm,
    gated_ref, value_ref, upstream_ref, dz_ref, rate_ref, gts, dzts, lam, pack, stage, sems, out_sems, dz_sems
):
    half = GROUP * LANES
    groups = blocks // GROUP
    start = pl.multiple_of(lax.axis_index("ch") * (blocks * LANES), LANES)
    rate_copy = pltpu.make_async_copy(
        rate_hbm.at[:, pl.ds(start, blocks * LANES)], rate_ref, sems.at[3 * groups]
    )
    copies = []
    for g in range(groups):
        rows = pl.ds(g * half, half)
        pairs = ((gated_hbm, gated_ref), (upstream_hbm, upstream_ref), (value_hbm, value_ref))
        copies.append(
            [
                pltpu.make_async_copy(src.at[rows, :], dst.at[rows, :], sems.at[3 * g + k])
                for k, (src, dst) in enumerate(pairs)
            ]
        )
    for copy in copies[0] + [rate_copy]:
        copy.start()
    copies[0][0].wait()
    for j in range(GROUP):
        put_signal(gated_ref, gts[0], j, j, tokens)
    copies[0][1].wait()
    copies[0][2].wait()
    for j in range(GROUP):
        put_dz(value_ref, upstream_ref, dz_ref, dzts[0], j, j, tokens)
    for part in copies[1:]:
        for copy in part:
            copy.start()
    rate_copy.wait()
    spread_modes(rate_ref, lam, 0, modes, blocks)
    zero = jnp.zeros((GROUP, LANES), F32)
    sent, late = [], []
    for g in range(groups):
        gt, dzt = gts[g], dzts[g]
        if g:
            for copy in copies[g]:
                copy.wait()
            for j in range(GROUP):
                put_signal(gated_ref, gt, g * GROUP + j, j, tokens)
                put_dz(value_ref, upstream_ref, dz_ref, dzt, g * GROUP + j, j, tokens)
        rows = pl.ds(g * half, half)
        copy = pltpu.make_async_copy(dz_ref.at[rows, :], dz_hbm.at[rows, :], dz_sems.at[g])
        copy.start()
        late.append(copy)
        lags = None
        for m0 in range(0, modes, STATE_PART):
            some = range(m0, m0 + STATE_PART)
            decay = [jnp.exp(-lam[tile(g * modes + m), :]) for m in some]
            jump = [power(a, RUN) for a in decay]

            def body(i, carry, gt=gt, dzt=dzt, decay=decay, jump=jump, first=m0 == 0):
                x, y, own, reach, lags = carry
                for u in range(STATE_UNROLL // RUN):
                    t = i * STATE_UNROLL + u * RUN
                    gs = [gt[tile(t + k), :] for k in range(RUN)]
                    ds = [dzt[tile(t + k), :] for k in range(RUN)]
                    if first:
                        lags = [
                            c + total([d * v for d, v in zip(ds[k:], gs)])
                            for k, c in enumerate(lags)
                        ]
                    ends = [horner(a, gs) for a in decay]
                    starts = [horner(a, ds[::-1]) for a in decay]
                    own = [o + v * w for o, v, w in zip(own, x, starts)]
                    y = [v + p * w for v, p, w in zip(y, reach, starts)]
                    x = [a * v + w for a, v, w in zip(jump, x, ends)]
                    reach = [a * p for a, p in zip(jump, reach)]
                return x, y, own, reach, lags

            zeros = [zero] * STATE_PART
            ones = [zero + 1.0] * STATE_PART
            carry = (zeros, zeros, zeros, ones, [zero] * RUN if m0 == 0 else [])
            x, y, own, _, found = lax.fori_loop(0, tokens // STATE_UNROLL, body, carry)
            lags = found if m0 == 0 else lags
            for k in range(STATE_PART):
                base = (m0 + k) * GROUP * 2 * KINDS + g * KINDS
                term = decay[k] * own[k] + horner(decay[k], lags[::-1])
                for kind, rows in enumerate((x[k], y[k], term)):
                    pack[pl.ds(base + kind, GROUP, stride=2 * KINDS), :] = rows
            if g < groups - 1:
                continue
            rows = pl.ds(m0 * GROUP * 2 * KINDS, STATE_PART * GROUP * 2 * KINDS)
            stage[rows, :] = pack[rows, :].astype(BF16)
            copy = pltpu.make_async_copy(
                stage.at[rows, :], out_hbm.at[rows, :], out_sems.at[len(sent)]
            )
            copy.start()
            sent.append(copy)
    for copy in sent + late:
        copy.wait()


def own_sums(modes, tokens, g, signal, out_ref, dec_ref, gain_ref, skip, order):
    zero = jnp.zeros((GROUP, LANES), F32)
    for m0 in range(0, modes, PART):
        decay = [dec_ref[tile(g * modes + m), :] for m in range(m0, m0 + PART)]
        gain = [gain_ref[tile(g * modes + m), :] for m in range(m0, m0 + PART)]

        def body(i, x, m0=m0, decay=decay, gain=gain):
            for u in range(UNROLL):
                t = order(i * UNROLL + u)
                at = tile(g * tokens + t)
                v = signal[tile(t), :]
                x = [a * w + v for a, w in zip(decay, x)]
                known = out_ref[at, :] if m0 else skip * v
                out_ref[at, :] = total([r * w for r, w in zip(gain, x)] + [known])
            return x

        lax.fori_loop(0, tokens // UNROLL, body, [zero] * PART)


def skip_of(skip_ref, first, g):
    parts = [
        skip_ref[:, pl.ds(pl.multiple_of(first + (g * GROUP + j) * LANES, LANES), LANES)]
        for j in range(GROUP)
    ]
    return jnp.concatenate(parts, axis=0)


def place_of(chip):
    z = chip % RUN_OF_CHIPS
    return ((8 - z) % 4 * 2 + z // 4) * RUN_OF_CHIPS + chip // RUN_OF_CHIPS


def ahead_kernel(
    modes, blocks, tokens, gated_ref, rate_ref, res_ref, skip_ref,
    fwd_ref, dec_ref, gain_ref, lam_ref, gt
):
    first = lax.axis_index("ch") * (blocks * LANES)
    spread_modes(rate_ref, dec_ref, first, modes, blocks)
    spread_modes(res_ref, gain_ref, first, modes, blocks)
    for h in range(2):
        for g in range(blocks // GROUP):
            chip = lax.axis_index("seq") // 2
            row = g * modes * GROUP + place_of(chip) * 2 + h
            own = dec_ref[pl.ds(row, 1), :]
            lam_ref[pl.ds(2 * h + g, 1), :] = own
    dec_ref[...] = jnp.exp(-dec_ref[...])
    for g in range(blocks // GROUP):
        for j in range(GROUP):
            put_signal(gated_ref, gt, g * GROUP + j, j, tokens)
        skip = skip_of(skip_ref, first, g)
        own_sums(modes, tokens, g, gt, fwd_ref, dec_ref, gain_ref, skip, lambda t: t)


def behind_kernel(modes, blocks, tokens, dz_ref, dec_ref, gain_ref, skip_ref, bwd_ref, dzt):
    first = lax.axis_index("ch") * (blocks * LANES)
    for g in range(blocks // GROUP):
        for j in range(GROUP):
            put_signal(dz_ref, dzt, g * GROUP + j, j, tokens)
        skip = skip_of(skip_ref, first, g)
        order = lambda t: tokens - 1 - t
        own_sums(modes, tokens, g, dzt, bwd_ref, dec_ref, gain_ref, skip, order)


def scan_kernel(chunks, tokens, own_ref, other_ref, lam_ref, out_ref, sums, outs):
    core = lax.axis_index("seq") % 2
    chips = chunks // 2
    sums[core] = own_ref[...].astype(F32)
    sums[1 - core] = other_ref[...].astype(F32)
    lam = lam_ref[...]
    step = jnp.exp(lam * (-1.0 * tokens))
    zero = jnp.zeros((4, LANES), F32)

    def at(q, kind):
        return pl.ds(q * 4 * KINDS + kind, 4, stride=KINDS)

    def body(i, carry):
        x, y, own, cross = carry
        for u in range(RUN_OF_CHIPS):
            q = place_of(u) + i
            r = place_of(RUN_OF_CHIPS - 1 - u) + RUN_OF_CHIPS - 1 - i
            for place in range(2):
                outs[place, at(q, 0), :] = x
                outs[1 - place, at(r, 1), :] = y
                own = own + sums[place, at(q, 2), :]
                cross = cross + sums[place, at(q, 1), :] * x
                x = step * x + sums[place, at(q, 0), :]
                y = step * y + sums[1 - place, at(r, 1), :]
        return x, y, own, cross

    _, _, own, cross = lax.fori_loop(0, RUN_OF_CHIPS, body, (zero, zero, zero, zero))
    grad = (own + cross * jnp.exp(-lam)) * (1.0 / (chunks * tokens))
    for q in range(chips):
        outs[core, at(q, 2), :] = grad
    out_ref[...] = outs[core].astype(BF16)


def residue_kernel(modes, blocks, in_ref, out_ref, wire_ref, tiles, flat):
    tiles[...] = in_ref[...].astype(F32)
    for r in range(modes * blocks // GROUP):
        base = r % modes * GROUP * 2 * KINDS + r // modes * KINDS
        flat[pl.ds(r * GROUP, GROUP), :] = tiles[pl.ds(base + 2, GROUP, stride=2 * KINDS), :]
    for b in range(blocks):
        row = b // GROUP * modes * GROUP + b % GROUP
        found = flat[pl.ds(row, modes, stride=GROUP), :]
        out_ref[:, pl.ds(b * LANES, LANES)] = found
        wire_ref[:, pl.ds(b * LANES, LANES)] = found.astype(BF16)


def final_kernel(
    modes, blocks, tokens, in_ref, fwd_ref, bwd_hbm, dec_ref, gain_ref, upstream_hbm, residue_ref,
    grad_gated_hbm, grad_value_hbm, grad_residue_hbm, tiles, zts, gts, bwd_ref, upstream_ref, grad_gated_ref,
    grad_value_ref, in_sems, sems
):
    groups = blocks // GROUP
    half = GROUP * LANES
    own_copies = []
    for g in range(groups):
        rows = pl.ds(g * tokens * GROUP, tokens * GROUP)
        own_copies.append(
            pltpu.make_async_copy(bwd_hbm.at[rows, :], bwd_ref.at[rows, :], in_sems.at[g])
        )
    upstream_copy = pltpu.make_async_copy(upstream_hbm, upstream_ref, in_sems.at[groups])
    channels = blocks * LANES
    start = pl.multiple_of(lax.axis_index("ch") * channels, LANES)
    residue_copy = pltpu.make_async_copy(
        residue_ref, grad_residue_hbm.at[:, pl.ds(start, channels)], in_sems.at[groups + 1]
    )
    for copy in [own_copies[0], upstream_copy] + own_copies[1:] + [residue_copy]:
        copy.start()
    tiles[...] = in_ref[...].astype(F32)
    copies = []

    def send(src, dst, first, size):
        rows = pl.ds(first * LANES, size * LANES)
        copy = pltpu.make_async_copy(src.at[rows, :], dst.at[rows, :], sems.at[len(copies)])
        copy.start()
        copies.append(copy)

    for g in range(groups):
        decay = [dec_ref[tile(g * modes + m), :] for m in range(modes)]
        scale = [gain_ref[tile(g * modes + m), :] * decay[m] for m in range(modes)]

        def entering(kind, g=g, scale=scale):
            bases = [m * GROUP * 2 * KINDS + g * KINDS + kind for m in range(modes)]
            return [
                tiles[pl.ds(base, GROUP, stride=2 * KINDS), :] * a for base, a in zip(bases, scale)
            ]

        def ahead(i, x, g=g, decay=decay):
            for u in range(FINAL_UNROLL):
                t = i * FINAL_UNROLL + u
                zts[g][tile(t), :] = fwd_ref[tile(g * tokens + t), :] + total(list(x))
                x = [a * v for a, v in zip(decay, x)]
            return x

        def behind(i, y, g=g, decay=decay):
            for u in range(FINAL_UNROLL):
                s = tokens - 1 - i * FINAL_UNROLL - u
                gts[g][tile(s), :] = bwd_ref[tile(g * tokens + s), :] + total(list(y))
                y = [a * v for a, v in zip(decay, y)]
            return y

        lax.fori_loop(0, tokens // FINAL_UNROLL, ahead, entering(0))
        if g == 0:
            upstream_copy.wait()
        for j in range(GROUP):
            rows = pl.ds(g * half + j * LANES, LANES)
            z = transposed(zts[g][pl.ds(j, tokens, stride=GROUP), :].astype(BF16))
            grad_value_ref[rows, :] = (upstream_ref[rows, :].astype(F32) * z).astype(BF16)
        send(grad_value_ref, grad_value_hbm, g * GROUP, GROUP)
        own_copies[g].wait()
        lax.fori_loop(0, tokens // FINAL_UNROLL, behind, entering(1))
        for j in range(GROUP):
            rows = pl.ds(g * half + j * LANES, LANES)
            back = transposed(gts[g][pl.ds(j, tokens, stride=GROUP), :].astype(BF16))
            grad_gated_ref[rows, :] = back.astype(BF16)
            if j == 3:
                send(grad_gated_ref, grad_gated_hbm, g * GROUP, 4)
            elif j in (5, 7):
                send(grad_gated_ref, grad_gated_hbm, g * GROUP + j - 1, 2)
    for copy in copies + [residue_copy]:
        copy.wait()


def local(gated, value, upstream, residue, rate, skip_weight):
    channels, tokens = gated.shape
    modes = rate.shape[1]
    chunks = lax.axis_size("seq")
    blocks = channels // LANES
    pairs = modes * blocks
    groups = blocks // GROUP
    assert tokens == LANES == UNROLL * GROUP and pairs == 2 * chunks
    assert blocks == 2 * GROUP and modes == 2 * PART and chunks == 2 * RUN_OF_CHIPS**2
    rate_t, residue_t, skip = rate.T, residue.T, skip_weight[None, :]
    vmem = pl.BlockSpec(memory_space=pltpu.VMEM)
    hbm = pl.BlockSpec(memory_space=pltpu.HBM)
    cells = modes * channels * tokens

    def call(kernel, specs, out_specs, shapes, scratch, flops, size, limit=16 * 2**20):
        return pl.pallas_call(
            kernel,
            in_specs=specs,
            out_specs=out_specs,
            out_shape=[jax.ShapeDtypeStruct(*shape) for shape in shapes],
            scratch_shapes=scratch,
            compiler_params=pltpu.CompilerParams(vmem_limit_bytes=limit),
            cost_estimate=pl.CostEstimate(flops=flops, bytes_accessed=size, transcendentals=0),
        )

    native = ((channels, tokens), BF16)
    signal = ((tokens * blocks, LANES), F32)
    per_mode = ((pairs, LANES), F32)
    wire = (chunks * 2 * KINDS, LANES)
    one = pltpu.VMEM((tokens * GROUP, LANES), F32)
    raw = pltpu.VMEM(*native)
    unpacked = pltpu.VMEM(wire, F32)
    staged = pltpu.VMEM(wire, BF16)
    flat = pltpu.VMEM(*per_mode)
    sems = lambda count: pltpu.SemaphoreType.DMA((count,))
    states, dz = call(
        functools.partial(state_kernel, modes, blocks, tokens),
        [hbm] * 4,
        [hbm] * 2,
        [(wire, BF16), native],
        [raw, raw, raw, raw, pltpu.VMEM((modes, channels), F32), [one] * groups, [one] * groups]
        + [flat, unpacked, staged, sems(3 * groups + 1), sems(modes // STATE_PART)]
        + [sems(groups)],
        5 * cells,
        8 * channels * tokens,
        LIMIT,
    )(gated, value, upstream, rate_t)

    def exchange(array):
        array = array.reshape(chunks // 2, KINDS, 4, LANES)
        by_place = sorted(range(chunks // 2), key=place_of)
        members = [[2 * chip + core for chip in by_place] for core in range(2)]
        return lax.all_to_all(
            array, "seq", split_axis=0, concat_axis=0, axis_index_groups=members, tiled=True
        ).reshape(wire)

    states, gated_held = lax.optimization_barrier((states, gated))
    fwd, decay, gain, lam = call(
        functools.partial(ahead_kernel, modes, blocks, tokens),
        [vmem] * 4,
        [vmem] * 4,
        [signal, per_mode, per_mode, ((4, LANES), F32)],
        [one],
        4 * cells,
        6 * channels * tokens,
    )(gated_held, rate_t, residue_t, skip)
    fwd, dz = lax.optimization_barrier((fwd, dz))
    (bwd,) = call(
        functools.partial(behind_kernel, modes, blocks, tokens),
        [vmem] * 4,
        [vmem],
        [signal],
        [one],
        4 * cells,
        6 * channels * tokens,
    )(dz, decay, gain, skip)
    heard, fwd, bwd, lam = lax.optimization_barrier((exchange(states), fwd, bwd, lam))
    heard_other = lax.ppermute(heard, "seq", [(d, d ^ 1) for d in range(chunks)])
    chained = pltpu.VMEM((2,) + wire, F32)
    (entering,) = call(
        functools.partial(scan_kernel, chunks, tokens),
        [vmem] * 3,
        [vmem],
        [(wire, BF16)],
        [chained, chained],
        16 * chunks * GROUP * LANES,
        8 * chunks * GROUP * LANES,
    )(heard, heard_other, lam)
    returned = exchange(entering)
    grad_own, grad_wire = call(
        functools.partial(residue_kernel, modes, blocks),
        [vmem],
        [vmem] * 2,
        [((modes, channels), F32), ((modes, channels), BF16)],
        [unpacked, flat],
        modes * channels,
        8 * modes * channels,
    )(returned)
    grad_other = lax.ppermute(grad_wire, "ch", [(0, 1), (1, 0)]).astype(F32)
    grad_gated, grad_value, grad_res = call(
        functools.partial(final_kernel, modes, blocks, tokens),
        [vmem, vmem, hbm, vmem, vmem, hbm, vmem],
        [hbm] * 3,
        [native, native, ((modes, residue.shape[0]), F32)],
        [unpacked, [one] * groups, [one] * groups, pltpu.VMEM(*signal), raw, raw, raw]
        + [sems(groups + 2), sems(4 * groups)],
        4 * cells,
        14 * channels * tokens,
    )(returned, fwd, bwd, decay, gain, upstream, grad_own)
    place = (1 - lax.axis_index("ch")) * channels
    grad_res = lax.dynamic_update_slice(grad_res, grad_other, (0, place))
    return (grad_gated, grad_value, grad_res.T)


def solution(mesh):
    return jax.shard_map(
        local,
        mesh=mesh,
        in_specs=(P("ch", "seq"), P("ch", "seq"), P("ch", "seq"), P(), P(), P()),
        out_specs=(P("ch", "seq"), P("ch", "seq"), P()),
        check_vma=False,
    )
```
